32 devices in a mesh: ax: 8 (over z, x), rad: 4 (over y, core).
Axes of the slice: x: 2, y: 2, z: 4, core: 2. Of those that a mesh axis runs over, the one named last changes fastest.
Arguments:
- forcing: float32 [32, 5, 128, 512], P(None, None, 'ax', 'rad'), may hold values from -300 to 300, as said below
- vel_axial: float32 [128, 512], P('ax', 'rad'), may hold values from 0.2 to 1
- vel_radial: float32 [128, 512], P('ax', 'rad'), may hold values from -0.4 to 0.4
- coupling: float32 [5, 5, 128, 512], P(None, None, 'ax', 'rad'), may hold values from -1.5 to 1.5
- viscosity: float32 [5], replicated, may hold values from 0.03 to 0.18
Outputs:
- basis: float32 [32, 5, 128, 512], P(None, None, 'ax', 'rad')
- r_factor: float32 [32, 32], replicated
The draws below stay inside these ranges and needn't reach their ends.
Inputs may be any that keep to these rules, and one draw needn't show every extreme that they name: `forcing`: forcing of the linearized equations.
All inputs are finite; a program needn't handle non-finite values.
Results may differ from the reference program's by a relative error of at most 0.00024.
Values sent between devices are 32-bit elements; how exact they have to be, the bound alone decides.
A program may use at most 64 MiB of HBM per device.

```python
import math
import jax
import jax.numpy as jnp
from jax import lax

K = 32
V = 5
STEPS = 3
NA = 128
NR = 512
ROWS = 327680


def draw_forcing(key, part):
    keys = jax.random.split(key, 4)
    axial = jnp.arange(NA, dtype=jnp.float32) / (NA - 1)
    own = jnp.clip(jax.random.normal(keys[0], (K, V, NA, NR), jnp.float32), -5.0, 5.0)
    common = jnp.clip(jax.random.normal(keys[1], (V, NA, NR), jnp.float32), -5.0, 5.0)
    weights = jax.random.uniform(keys[2], (K,), jnp.float32, 0.4, 0.8)
    envelope = 1.0 + 2.0 * axial
    scales = 10.0 ** jax.random.uniform(keys[3], (K,), jnp.float32, 0.0, 1.0)
    field = (own + weights[:, None, None, None] * common[None]) * envelope[None, None, :, None]
    field = field * scales[:, None, None, None]
    return field.astype(jnp.float32)


def block_levels(key, extent, pieces, least, high):
    def one(dim, shards_of):
        heights = jax.random.uniform(jax.random.fold_in(jax.random.fold_in(key, 6), dim), (shards_of,), jnp.float32, least / len(pieces), high / len(pieces))
        return jnp.repeat(jnp.exp(heights), extent[dim] // shards_of).reshape((-1,) + (1,) * (len(extent) - dim - 1))

    loudness = one(*pieces[0])
    for cut in pieces[1:]:
        loudness = loudness * one(*cut)
    return loudness


def centred(key, dims, deviation, limit, cuts=(), kind=jnp.bfloat16):
    values = jax.random.normal(key, dims, jnp.float32) * deviation
    if len(cuts) > 0:
        values = block_levels(key, dims, cuts, -0.22, 0.18) * values
    return jnp.clip(values, min=-limit, max=limit).astype(kind)


def setup_inputs(seed: int = 0) -> dict:
    arg_keys = jax.random.split(jax.random.key(seed), 6)
    forcing = draw_forcing(jax.random.fold_in(arg_keys[5], 71), 0)
    vel_axial = jnp.clip(0.2 + 0.8 * jax.random.uniform(arg_keys[1], (NA, NR), jnp.float32) ** block_levels(arg_keys[1], (NA, NR), ((0, 8), (1, 4)), -0.2, 0.2), 0.2, 1.0)
    vel_radial = jnp.clip(jax.random.uniform(arg_keys[2], (NA, NR), jnp.float32, -0.4, 0.4) * block_levels(arg_keys[2], (NA, NR), ((0, 8), (1, 4)), -0.4, 0.0), -0.4, 0.4)
    coupling = centred(arg_keys[3], (V, V, NA, NR), 0.3, 1.5, ((2, 8), (3, 4)), jnp.float32)
    viscosity = jnp.clip(jnp.exp(jax.random.uniform(arg_keys[4], (V,), jnp.float32, math.log(0.03), math.log(0.18))), 0.03, 0.18)
    return dict(forcing=forcing, vel_axial=vel_axial, vel_radial=vel_radial, coupling=coupling, viscosity=viscosity)


time_step = 0.8

def operate(padded, vel_axial, vel_radial, coupling, viscosity):
    center = padded[..., 2:-2, 2:-2]
    axial_up = padded[..., 3:-1, 2:-2]
    axial_down = padded[..., 1:-3, 2:-2]
    axial_far_up = padded[..., 4:, 2:-2]
    axial_far_down = padded[..., :-4, 2:-2]
    radial_up = padded[..., 2:-2, 3:-1]
    radial_down = padded[..., 2:-2, 1:-3]
    radial_far_up = padded[..., 2:-2, 4:]
    radial_far_down = padded[..., 2:-2, :-4]
    first_axial = (8.0 * (axial_up - axial_down) - (axial_far_up - axial_far_down)) / 12.0
    first_radial = (8.0 * (radial_up - radial_down) - (radial_far_up - radial_far_down)) / 12.0
    second = (16.0 * (axial_up + axial_down + radial_up + radial_down) - (axial_far_up + axial_far_down + radial_far_up + radial_far_down) - 60.0 * center) / 12.0
    result = -vel_axial * first_axial - vel_radial * first_radial + viscosity[:, None, None] * second
    for source in range(coupling.shape[1]):
        result = result + coupling[:, source] * center[..., source:source + 1, :, :]
    return result

def upper_inverse(upper_factor):
    order = upper_factor.shape[0]
    identity = jnp.eye(order, dtype=jnp.float32)

    def one_row(count, inverse):
        row_index = order - 1 - count
        factor_row = lax.dynamic_slice_in_dim(upper_factor, row_index, 1, 0)
        unit_row = lax.dynamic_slice_in_dim(identity, row_index, 1, 0)
        pivot = jnp.sum(factor_row * unit_row)
        new_row = (unit_row - jnp.dot(factor_row, inverse, precision=lax.Precision.HIGHEST)) / pivot
        return lax.dynamic_update_slice_in_dim(inverse, new_row, row_index, 0)
    return lax.fori_loop(0, order, one_row, jnp.zeros((order, order), jnp.float32))

def reference(forcing, vel_axial, vel_radial, coupling, viscosity):

    def apply_operator(field):
        padded = jnp.pad(field, ((0, 0), (2, 2), (2, 2)))
        return operate(padded, vel_axial, vel_radial, coupling, viscosity)

    def advance(vector):
        field_now = vector
        for step_index in range(STEPS):
            slope_one = apply_operator(field_now)
            middle = field_now + time_step * slope_one
            slope_two = apply_operator(middle)
            field_now = field_now + 0.5 * time_step * (slope_one + slope_two)
        return field_now
    response = lax.map(advance, forcing)
    flattened = response.reshape(K, ROWS)
    gram = jnp.dot(flattened, flattened.T, precision=lax.Precision.HIGHEST) / ROWS
    upper_factor = jnp.linalg.cholesky(gram).T
    inverse = upper_inverse(upper_factor)
    basis = jnp.dot(inverse.T, flattened, precision=lax.Precision.HIGHEST).reshape(response.shape)
    return (basis, upper_factor)
```

```python
import functools

import jax
import jax.numpy as jnp
from jax import lax
from jax.experimental import pallas as pl
from jax.experimental.pallas import tpu as pltpu
from jax.sharding import PartitionSpec as P

STEPS = 3
time_step = 0.8

LANES = 128
SUB = 8
MESH = pl.DeviceIdType.MESH


def kernel(
    sizes, f_ref, va_ref, vr_ref, cp_ref, nu_ref, out_ref, r_ref,
    field, coef, packed, from_left, from_right, split, mine, rad_slots, ax_slots,
    send_sem, recv_sem, rad_send, rad_recv, ax_send, ax_recv,
):
    vectors, variables, rows, n_ax, n_rad = sizes
    groups = vectors // SUB
    cells = variables * rows
    ax = lax.axis_index("ax")
    rad = lax.axis_index("rad")
    ax_before = lax.rem(ax + n_ax - 1, n_ax)
    ax_after = lax.rem(ax + 1, n_ax)
    rad_before = lax.rem(rad + n_rad - 1, n_rad)
    rad_after = lax.rem(rad + 1, n_rad)
    sends = (ax > 0, ax < n_ax - 1, rad > 0, rad < n_rad - 1)
    takes = (ax < n_ax - 1, ax > 0, rad < n_rad - 1, rad > 0)
    lane = lax.broadcasted_iota(jnp.int32, (SUB, LANES), 1)
    sub = lax.broadcasted_iota(jnp.int32, (SUB, LANES), 0)
    slot = lane // 8
    tile = (SUB, LANES)

    def link(buf, g, d):
        if d == 0:
            src, dst = field.at[buf, g, :, 2:4], field.at[buf, g, :, rows + 2 : rows + 4]
            device = (ax_before, rad)
        elif d == 1:
            src, dst = field.at[buf, g, :, rows : rows + 2], field.at[buf, g, :, 0:2]
            device = (ax_after, rad)
        elif d == 2:
            src, dst = packed.at[buf, g], from_right.at[buf, g]
            device = (ax, rad_before)
        else:
            src, dst = packed.at[buf, g], from_left.at[buf, g]
            device = (ax, rad_after)
        return pltpu.make_async_remote_copy(
            src_ref=src, dst_ref=dst,
            send_sem=send_sem.at[buf, g, d], recv_sem=recv_sem.at[buf, g, d],
            device_id=device, device_id_type=MESH,
        )

    def start(buf, g, d):
        @pl.when(sends[d])
        def _():
            link(buf, g, d).start()

    def wait_send(buf, g, d):
        @pl.when(sends[d])
        def _():
            link(buf, g, d).wait_send()

    def wait_recv(buf, g, d):
        @pl.when(takes[d])
        def _():
            link(buf, g, d).wait_recv()

    zero_rows = jnp.zeros((variables, 2, SUB, LANES), jnp.float32)
    zero_side = jnp.zeros((variables, SUB, LANES), jnp.float32)
    for buf in range(2):
        for g in range(groups):
            field[buf, g, :, 0:2] = zero_rows
            field[buf, g, :, rows + 2 : rows + 4] = zero_rows
            from_left[buf, g] = zero_side
            from_right[buf, g] = zero_side

    barrier = pltpu.get_barrier_semaphore()
    for step in range(1, n_ax):
        pl.semaphore_signal(
            barrier, inc=1, device_id=(lax.rem(ax + step, n_ax), rad), device_id_type=MESH
        )
    for step in range(1, n_rad):
        pl.semaphore_signal(
            barrier, inc=1, device_id=(ax, lax.rem(rad + step, n_rad)), device_id_type=MESH
        )

    def bring(g, carry):
        for v in range(variables):
            pack = jnp.zeros(tile, jnp.float32)
            for a in range(rows):
                value = f_ref[pl.ds(g * (SUB * cells) + v * rows + a, SUB, stride=cells), :]
                field[0, g, v, a + 2] = value
                pack = jnp.where(slot == a, pltpu.roll(value, 2 + 8 * a, 1), pack)
            packed[0, g, v] = pack
        return carry

    lax.fori_loop(0, groups, bring, 0)
    pl.semaphore_wait(barrier, n_ax + n_rad - 2)

    def send_first(g, carry):
        for d in range(4):
            start(0, g, d)
        return carry

    lax.fori_loop(0, groups, send_first, 0)

    def prepare(a, carry):
        vel_a = jnp.broadcast_to(va_ref[pl.ds(a, 1), :], tile) * (time_step / 12.0)
        vel_r = jnp.broadcast_to(vr_ref[pl.ds(a, 1), :], tile) * (time_step / 12.0)
        for v in range(variables):
            nu = jnp.full(tile, nu_ref[v], jnp.float32) * (time_step / 12.0)
            terms = []
            for vel in (vel_a, vel_r):
                terms += [16.0 * nu - 8.0 * vel, 16.0 * nu + 8.0 * vel, vel - nu, -vel - nu]
            for w in range(variables):
                term = time_step * jnp.broadcast_to(cp_ref[v, w, pl.ds(a, 1), :], tile)
                if w == v:
                    term = term + (1.0 - 60.0 * nu)
                terms.append(term)
            for t, term in enumerate(terms):
                coef[v, a, t] = term
        return carry

    lax.fori_loop(0, rows, prepare, 0)

    def advance(src, g, start_axial):
        dst = 1 - src
        sides = [
            jnp.where(lane % 8 < 2, from_left[src, g, v], from_right[src, g, v])
            for v in range(variables)
        ]
        packs = [jnp.zeros(tile, jnp.float32) for _ in range(variables)]
        order = [0, 1, rows - 2, rows - 1] + list(range(2, rows - 2))
        for count, a in enumerate(order):
            centre = [field[src, g, v, a + 2] for v in range(variables)]
            for v in range(variables):
                x = centre[v]
                side = pltpu.roll(sides[v], (2 * LANES - 2 - 8 * a) % LANES, 1)
                near = [
                    field[src, g, v, a + 3],
                    field[src, g, v, a + 1],
                    field[src, g, v, a + 4],
                    field[src, g, v, a],
                    pltpu.roll(jnp.where(lane == 0, side, x), LANES - 1, 1),
                    pltpu.roll(jnp.where(lane == LANES - 1, side, x), 1, 1),
                    pltpu.roll(jnp.where(lane < 2, side, x), LANES - 2, 1),
                    pltpu.roll(jnp.where(lane >= LANES - 2, side, x), 2, 1),
                ]
                parts = [coef[v, a, t] * q for t, q in enumerate(near + centre)]
                while len(parts) > 1:
                    parts = [
                        parts[i] + parts[i + 1] if i + 1 < len(parts) else parts[i]
                        for i in range(0, len(parts), 2)
                    ]
                new = parts[0]
                if src == 1:
                    new = 0.5 * (field[dst, g, v, a + 2] + new)
                field[dst, g, v, a + 2] = new
                packs[v] = jnp.where(slot == a, pltpu.roll(new, 2 + 8 * a, 1), packs[v])
            if count == 3:
                start_axial()
        for v in range(variables):
            packed[dst, g, v] = packs[v]

    def both_halves(step, carry):
        def half(src):
            more = jnp.logical_or(step < STEPS - 1, src == 0)

            def one_group(g, inner):
                for d in range(4):
                    wait_recv(src, g, d)
                for d in range(4):
                    wait_send(src, g, d)

                def send(directions):
                    @pl.when(more)
                    def _():
                        for d in directions:
                            start(1 - src, g, d)

                advance(src, g, lambda: send((0, 1)))
                send((2, 3))
                return inner

            lax.fori_loop(0, groups, one_group, 0)

        half(0)
        half(1)
        return carry

    lax.fori_loop(0, STEPS, both_halves, 0)

    def products(v, total):
        for p in range(rows // 2):
            for e in range(2):
                x = jnp.concatenate(
                    [field[0, g, v, 2 * p + e + 2] for g in range(groups)], axis=0
                )
                high = x.astype(jnp.bfloat16)
                low = (x - high.astype(jnp.float32)).astype(jnp.bfloat16)
                split[v, p, :, e * LANES : (e + 1) * LANES] = jnp.concatenate(
                    [high, low, high, low], axis=0
                )
            both = split[v, p]
            total = total + lax.dot_general(
                both[: 2 * vectors], both, (((1,), (1,)), ((), ())),
                preferred_element_type=jnp.float32,
            )
        return total

    total = lax.fori_loop(
        0, variables, products, jnp.zeros((2 * vectors, LANES), jnp.float32)
    )
    half_sum = total[:vectors] + total[vectors:]
    gram = half_sum + pltpu.roll(half_sum, vectors, 1)
    gram = gram * (1.0 / (cells * LANES * n_ax * n_rad))
    quarter = lane // vectors
    folded = gram[:SUB]
    for i in range(1, vectors // SUB):
        folded = jnp.where(quarter == i, gram[SUB * i : SUB * (i + 1)], folded)

    def sum_over(value, n, me, place, slots, sends_on, takes_on, held):
        held[...] = value
        copies = []
        for step in range(1, n):
            copy = pltpu.make_async_remote_copy(
                src_ref=held, dst_ref=slots.at[me],
                send_sem=sends_on.at[step], recv_sem=takes_on.at[step],
                device_id=place(lax.rem(me + step, n)), device_id_type=MESH,
            )
            copy.start()
            copies.append(copy)
        slots[me] = value
        for copy in copies:
            copy.wait_send()
            copy.wait_recv()
        result = slots[0]
        for i in range(1, n):
            result = result + slots[i]
        return result

    folded = sum_over(
        folded, n_rad, rad, lambda i: (ax, i), rad_slots, rad_send, rad_recv, mine.at[0]
    )
    folded = sum_over(
        folded, n_ax, ax, lambda i: (i, rad), ax_slots, ax_send, ax_recv, mine.at[1]
    )

    blocks = []
    for b in range(vectors // SUB):
        part = folded if b == 0 else pltpu.roll(folded, LANES - vectors * b, 1)
        unit = jnp.where(lane - vectors == sub + SUB * b, 1.0, 0.0)
        blocks.append(jnp.where(lane < vectors, part, unit))
    for j in range(vectors):
        jb, js = j // SUB, j % SUB
        row = jnp.broadcast_to(blocks[jb][js : js + 1, :], tile)
        columns = {
            b: jnp.broadcast_to(blocks[b][:, j : j + 1], tile) for b in range(jb, len(blocks))
        }
        pivot = jnp.broadcast_to(columns[jb][js : js + 1, :], tile)
        scaled = row * (1.0 / pivot)
        for b in range(jb, len(blocks)):
            change = columns[b] * scaled
            if b == jb:
                change = jnp.where(sub > js, change, 0.0)
            blocks[b] = blocks[b] - change
    lefts, rights = [], []
    for b, block in enumerate(blocks):
        diagonal = jnp.sum(
            jnp.where(lane == sub + SUB * b, block, 0.0), axis=1, keepdims=True
        )
        block = block * (1.0 / jnp.sqrt(jnp.broadcast_to(diagonal, tile)))
        lefts.append(jnp.where(lane >= sub + SUB * b, block, 0.0))
        inverse = jnp.where(quarter == 1, block, 0.0)
        inverse = inverse + pltpu.roll(inverse, vectors, 1)
        inverse = inverse + pltpu.roll(inverse, 2 * vectors, 1)
        rights.append(inverse)
    r_ref[...] = jnp.concatenate(lefts, axis=0)[:, :vectors]
    inverse = jnp.concatenate(rights, axis=0)
    high = inverse.astype(jnp.bfloat16).astype(jnp.float32)
    wide = lax.broadcasted_iota(jnp.int32, (vectors, LANES), 1)
    factors = jnp.where(wide < 2 * vectors, high, inverse - high).astype(jnp.bfloat16)

    def outputs(v, carry):
        for p in range(rows // 2):
            found = jnp.dot(factors, split[v, p], preferred_element_type=jnp.float32)
            for e in range(2):
                out_ref[pl.ds(v * rows + 2 * p + e, vectors, stride=cells), :] = found[
                    :, e * LANES : (e + 1) * LANES
                ]
        return carry

    lax.fori_loop(0, variables, outputs, 0)


def per_device(forcing, vel_axial, vel_radial, coupling, viscosity):
    vectors, variables, rows, columns = forcing.shape
    n_ax, n_rad = lax.axis_size("ax"), lax.axis_size("rad")
    groups = vectors // SUB
    cells = variables * rows
    assert columns == LANES and rows * 8 == LANES and vectors * 4 == LANES
    f32 = jnp.float32
    vmem = pl.BlockSpec(memory_space=pltpu.VMEM)
    side = pltpu.VMEM((2, groups, variables, SUB, LANES), f32)
    dma = pltpu.SemaphoreType.DMA
    basis, upper = pl.pallas_call(
        functools.partial(kernel, (vectors, variables, rows, n_ax, n_rad)),
        out_shape=(
            jax.ShapeDtypeStruct((vectors * cells, LANES), f32),
            jax.ShapeDtypeStruct((vectors, vectors), f32),
        ),
        in_specs=[vmem, vmem, vmem, vmem, pl.BlockSpec(memory_space=pltpu.SMEM)],
        out_specs=(vmem, vmem),
        scratch_shapes=[
            pltpu.VMEM((2, groups, variables, rows + 4, SUB, LANES), f32),
            pltpu.VMEM((variables, rows, 8 + variables, SUB, LANES), f32),
            side, side, side,
            pltpu.VMEM((variables, rows // 2, LANES, 2 * LANES), jnp.bfloat16),
            pltpu.VMEM((2, SUB, LANES), f32),
            pltpu.VMEM((n_rad, SUB, LANES), f32),
            pltpu.VMEM((n_ax, SUB, LANES), f32),
            dma((2, groups, 4)), dma((2, groups, 4)),
            dma((n_rad,)), dma((n_rad,)), dma((n_ax,)), dma((n_ax,)),
        ],
        compiler_params=pltpu.CompilerParams(
            collective_id=0, has_side_effects=True, vmem_limit_bytes=48 * 2**20
        ),
    )(forcing.reshape(vectors * cells, LANES), vel_axial, vel_radial, coupling, viscosity)
    return basis.reshape(forcing.shape), upper


def solution(mesh):
    return jax.shard_map(
        per_device,
        mesh=mesh,
        in_specs=(
            P(None, None, "ax", "rad"),
            P("ax", "rad"),
            P("ax", "rad"),
            P(None, None, "ax", "rad"),
            P(),
        ),
        out_specs=(P(None, None, "ax", "rad"), P()),
        check_vma=False,
    )
```

```python
import functools

import jax
import jax.numpy as jnp
from jax import lax
from jax.experimental import pallas as pl
from jax.experimental.pallas import tpu as pltpu
from jax.sharding import PartitionSpec as P

STEPS = 3
time_step = 0.8

LANES = 128
SUB = 8
MESH = pl.DeviceIdType.MESH


def kernel(
    sizes, f_ref, va_ref, vr_ref, cp_ref, nu_ref, out_ref, r_ref,
    forcing_in, va_in, vr_in, cp_in, nu_in, in_sem,
    field_0, field_1, coef, packed, from_left, from_right, split, mine, rad_slots, ax_slots,
    send_sem, recv_sem, rad_send, rad_recv, ax_send, ax_recv,
):
    vectors, variables, rows, n_ax, n_rad = sizes
    groups = vectors // SUB
    cells = variables * rows
    fields = (field_0, field_1)
    ax = lax.axis_index("ax")
    rad = lax.axis_index("rad")
    ax_before = lax.rem(ax + n_ax - 1, n_ax)
    ax_after = lax.rem(ax + 1, n_ax)
    rad_before = lax.rem(rad + n_rad - 1, n_rad)
    rad_after = lax.rem(rad + 1, n_rad)
    sends = (ax > 0, ax < n_ax - 1, rad > 0, rad < n_rad - 1)
    takes = (ax < n_ax - 1, ax > 0, rad < n_rad - 1, rad > 0)
    lane = lax.broadcasted_iota(jnp.int32, (SUB, LANES), 1)
    sub = lax.broadcasted_iota(jnp.int32, (SUB, LANES), 0)
    slot = lane // 8
    tile = (SUB, LANES)

    def link(buf, g, d):
        if d == 0:
            src, dst = fields[buf].at[g, :, 2:4], fields[buf].at[g, :, rows + 2 : rows + 4]
            device = (ax_before, rad)
        elif d == 1:
            src, dst = fields[buf].at[g, :, rows : rows + 2], fields[buf].at[g, :, 0:2]
            device = (ax_after, rad)
        elif d == 2:
            src, dst = packed.at[buf, g], from_right.at[buf, g]
            device = (ax, rad_before)
        else:
            src, dst = packed.at[buf, g], from_left.at[buf, g]
            device = (ax, rad_after)
        return pltpu.make_async_remote_copy(
            src_ref=src, dst_ref=dst,
            send_sem=send_sem.at[buf, g, d], recv_sem=recv_sem.at[buf, g, d],
            device_id=device, device_id_type=MESH,
        )

    def start(buf, g, d):
        @pl.when(sends[d])
        def _():
            link(buf, g, d).start()

    def wait_send(buf, g, d):
        @pl.when(sends[d])
        def _():
            link(buf, g, d).wait_send()

    def wait_recv(buf, g, d):
        @pl.when(takes[d])
        def _():
            link(buf, g, d).wait_recv()

    part = SUB * cells
    pieces = [
        pltpu.make_async_copy(
            f_ref.at[pl.ds(g * part, part)], forcing_in.at[pl.ds(g * part, part)], in_sem.at[g]
        )
        for g in range(groups)
    ]
    others = [
        pltpu.make_async_copy(source, target, in_sem.at[groups + i])
        for i, (source, target) in enumerate(
            ((va_ref, va_in), (vr_ref, vr_in), (cp_ref, cp_in), (nu_ref, nu_in))
        )
    ]
    for copy in pieces + others:
        copy.start()

    zero_rows = jnp.zeros((variables, 2, SUB, LANES), jnp.float32)
    zero_side = jnp.zeros((variables, SUB, LANES), jnp.float32)
    for buf in range(2):
        for g in range(groups):
            fields[buf][g, :, 0:2] = zero_rows
            fields[buf][g, :, rows + 2 : rows + 4] = zero_rows
            from_left[buf, g] = zero_side
            from_right[buf, g] = zero_side

    barrier = pltpu.get_barrier_semaphore()
    for step in range(1, n_ax):
        pl.semaphore_signal(
            barrier, inc=1, device_id=(lax.rem(ax + step, n_ax), rad), device_id_type=MESH
        )
    for step in range(1, n_rad):
        pl.semaphore_signal(
            barrier, inc=1, device_id=(ax, lax.rem(rad + step, n_rad)), device_id_type=MESH
        )

    for g in range(groups):
        pieces[g].wait()
        for v in range(variables):
            pack = jnp.zeros(tile, jnp.float32)
            for a in range(rows):
                value = forcing_in[pl.ds(g * part + v * rows + a, SUB, stride=cells), :]
                field_0[g, v, a + 2] = value
                pack = jnp.where(slot == a, pltpu.roll(value, 2 + 8 * a, 1), pack)
            packed[0, g, v] = pack
        if g == 0:
            pl.semaphore_wait(barrier, n_ax + n_rad - 2)
        for d in range(4):
            start(0, g, d)
    for copy in others:
        copy.wait()

    def prepare(a, carry):
        vel_a = jnp.broadcast_to(va_in[pl.ds(a, 1), :], tile) * (time_step / 12.0)
        vel_r = jnp.broadcast_to(vr_in[pl.ds(a, 1), :], tile) * (time_step / 12.0)
        for v in range(variables):
            nu = jnp.full(tile, nu_in[v], jnp.float32) * (time_step / 12.0)
            terms = []
            for vel in (vel_a, vel_r):
                terms += [16.0 * nu - 8.0 * vel, 16.0 * nu + 8.0 * vel, vel - nu, -vel - nu]
            for w in range(variables):
                term = time_step * jnp.broadcast_to(cp_in[v, w, pl.ds(a, 1), :], tile)
                if w == v:
                    term = term + (1.0 - 60.0 * nu)
                terms.append(term)
            for t, term in enumerate(terms):
                coef[v, a, t] = term
        return carry

    lax.fori_loop(0, rows, prepare, 0)

    def advance(src, g, start_axial):
        dst = 1 - src
        now, later = fields[src], fields[dst]
        held = []

        def store(keep):
            while len(held) > keep:
                v, a, value = held.pop(0)
                later[g, v, a + 2] = value

        sides = [
            jnp.where(lane % 8 < 2, from_left[src, g, v], from_right[src, g, v])
            for v in range(variables)
        ]
        packs = [jnp.zeros(tile, jnp.float32) for _ in range(variables)]
        order = [0, 1, rows - 2, rows - 1] + list(range(2, rows - 2))
        for count, a in enumerate(order):
            centre = [now[g, v, a + 2] for v in range(variables)]
            for v in range(variables):
                x = centre[v]
                side = pltpu.roll(sides[v], (2 * LANES - 2 - 8 * a) % LANES, 1)
                near = [
                    now[g, v, a + 3],
                    now[g, v, a + 1],
                    now[g, v, a + 4],
                    now[g, v, a],
                    pltpu.roll(jnp.where(lane == 0, side, x), LANES - 1, 1),
                    pltpu.roll(jnp.where(lane == LANES - 1, side, x), 1, 1),
                    pltpu.roll(jnp.where(lane < 2, side, x), LANES - 2, 1),
                    pltpu.roll(jnp.where(lane >= LANES - 2, side, x), 2, 1),
                ]
                parts = [coef[v, a, t] * q for t, q in enumerate(near + centre)]
                while len(parts) > 1:
                    parts = [
                        parts[i] + parts[i + 1] if i + 1 < len(parts) else parts[i]
                        for i in range(0, len(parts), 2)
                    ]
                new = parts[0]
                if src == 1:
                    new = 0.5 * (later[g, v, a + 2] + new)
                held.append((v, a, new))
                packs[v] = jnp.where(slot == a, pltpu.roll(new, 2 + 8 * a, 1), packs[v])
            if count == 3:
                store(0)
                start_axial()
            store(2 * variables)
        store(0)
        for v in range(variables):
            packed[dst, g, v] = packs[v]

    def both_halves(step, carry):
        def half(src):
            more = jnp.logical_or(step < STEPS - 1, src == 0)

            def one_group(g, inner):
                for d in range(4):
                    wait_recv(src, g, d)
                for d in range(4):
                    wait_send(src, g, d)

                def send(directions):
                    @pl.when(more)
                    def _():
                        for d in directions:
                            start(1 - src, g, d)

                advance(src, g, lambda: send((0, 1)))
                send((2, 3))
                return inner

            lax.fori_loop(0, groups, one_group, 0)

        half(0)
        half(1)
        return carry

    lax.fori_loop(0, STEPS, both_halves, 0)

    def products(v, total):
        for p in range(rows // 2):
            for e in range(2):
                x = jnp.concatenate(
                    [field_0[g, v, 2 * p + e + 2] for g in range(groups)], axis=0
                )
                high = x.astype(jnp.bfloat16)
                low = (x - high.astype(jnp.float32)).astype(jnp.bfloat16)
                split[v, p, :, e * LANES : (e + 1) * LANES] = jnp.concatenate(
                    [high, low, high, low], axis=0
                )
            both = split[v, p]
            total = total + lax.dot_general(
                both[: 2 * vectors], both, (((1,), (1,)), ((), ())),
                preferred_element_type=jnp.float32,
            )
        return total

    total = lax.fori_loop(
        0, variables, products, jnp.zeros((2 * vectors, LANES), jnp.float32)
    )
    half_sum = total[:vectors] + total[vectors:]
    gram = half_sum + pltpu.roll(half_sum, vectors, 1)
    gram = gram * (1.0 / (cells * LANES * n_ax * n_rad))
    quarter = lane // vectors
    folded = gram[:SUB]
    for i in range(1, vectors // SUB):
        folded = jnp.where(quarter == i, gram[SUB * i : SUB * (i + 1)], folded)

    def sum_over(value, n, me, place, slots, sends_on, takes_on, held):
        held[...] = value
        copies = []
        for step in range(1, n):
            copy = pltpu.make_async_remote_copy(
                src_ref=held, dst_ref=slots.at[me],
                send_sem=sends_on.at[step], recv_sem=takes_on.at[step],
                device_id=place(lax.rem(me + step, n)), device_id_type=MESH,
            )
            copy.start()
            copies.append(copy)
        slots[me] = value
        for copy in copies:
            copy.wait_send()
            copy.wait_recv()
        result = slots[0]
        for i in range(1, n):
            result = result + slots[i]
        return result

    folded = sum_over(
        folded, n_rad, rad, lambda i: (ax, i), rad_slots, rad_send, rad_recv, mine.at[0]
    )
    folded = sum_over(
        folded, n_ax, ax, lambda i: (i, rad), ax_slots, ax_send, ax_recv, mine.at[1]
    )

    blocks = []
    for b in range(vectors // SUB):
        part = folded if b == 0 else pltpu.roll(folded, LANES - vectors * b, 1)
        unit = jnp.where(lane - vectors == sub + SUB * b, 1.0, 0.0)
        blocks.append(jnp.where(lane < vectors, part, unit))
    for j in range(vectors):
        jb, js = j // SUB, j % SUB
        row = jnp.broadcast_to(blocks[jb][js : js + 1, :], tile)
        columns = {
            b: jnp.broadcast_to(blocks[b][:, j : j + 1], tile) for b in range(jb, len(blocks))
        }
        pivot = jnp.broadcast_to(columns[jb][js : js + 1, :], tile)
        scaled = row * (1.0 / pivot)
        for b in range(jb, len(blocks)):
            change = columns[b] * scaled
            if b == jb:
                change = jnp.where(sub > js, change, 0.0)
            blocks[b] = blocks[b] - change
    lefts, rights = [], []
    for b, block in enumerate(blocks):
        diagonal = jnp.sum(
            jnp.where(lane == sub + SUB * b, block, 0.0), axis=1, keepdims=True
        )
        block = block * (1.0 / jnp.sqrt(jnp.broadcast_to(diagonal, tile)))
        lefts.append(jnp.where(lane >= sub + SUB * b, block, 0.0))
        inverse = jnp.where(quarter == 1, block, 0.0)
        inverse = inverse + pltpu.roll(inverse, vectors, 1)
        inverse = inverse + pltpu.roll(inverse, 2 * vectors, 1)
        rights.append(inverse)
    r_ref[...] = jnp.concatenate(lefts, axis=0)[:, :vectors]
    inverse = jnp.concatenate(rights, axis=0)
    high = inverse.astype(jnp.bfloat16).astype(jnp.float32)
    wide = lax.broadcasted_iota(jnp.int32, (vectors, LANES), 1)
    factors = jnp.where(wide < 2 * vectors, high, inverse - high).astype(jnp.bfloat16)

    def outputs(v, carry):
        for p in range(rows // 2):
            found = jnp.dot(factors, split[v, p], preferred_element_type=jnp.float32)
            for e in range(2):
                out_ref[pl.ds(v * rows + 2 * p + e, vectors, stride=cells), :] = found[
                    :, e * LANES : (e + 1) * LANES
                ]
        return carry

    lax.fori_loop(0, variables, outputs, 0)


def per_device(forcing, vel_axial, vel_radial, coupling, viscosity):
    vectors, variables, rows, columns = forcing.shape
    n_ax, n_rad = lax.axis_size("ax"), lax.axis_size("rad")
    groups = vectors // SUB
    cells = variables * rows
    assert columns == LANES and rows * 8 == LANES and vectors * 4 == LANES
    f32 = jnp.float32
    vmem = pl.BlockSpec(memory_space=pltpu.VMEM)
    side = pltpu.VMEM((2, groups, variables, SUB, LANES), f32)
    field = pltpu.VMEM((groups, variables, rows + 4, SUB, LANES), f32)
    dma = pltpu.SemaphoreType.DMA
    basis, upper = pl.pallas_call(
        functools.partial(kernel, (vectors, variables, rows, n_ax, n_rad)),
        out_shape=(
            jax.ShapeDtypeStruct((vectors * cells, LANES), f32),
            jax.ShapeDtypeStruct((vectors, vectors), f32),
        ),
        in_specs=[pl.BlockSpec(memory_space=pl.ANY)] * 5,
        out_specs=(vmem, vmem),
        scratch_shapes=[
            pltpu.VMEM((vectors * cells, LANES), f32),
            pltpu.VMEM((rows, LANES), f32),
            pltpu.VMEM((rows, LANES), f32),
            pltpu.VMEM((variables, variables, rows, LANES), f32),
            pltpu.SMEM((variables,), f32),
            dma((groups + 4,)),
            field, field,
            pltpu.VMEM((variables, rows, 8 + variables, SUB, LANES), f32),
            side, side, side,
            pltpu.VMEM((variables, rows // 2, LANES, 2 * LANES), jnp.bfloat16),
            pltpu.VMEM((2, SUB, LANES), f32),
            pltpu.VMEM((n_rad, SUB, LANES), f32),
            pltpu.VMEM((n_ax, SUB, LANES), f32),
            dma((2, groups, 4)), dma((2, groups, 4)),
            dma((n_rad,)), dma((n_rad,)), dma((n_ax,)), dma((n_ax,)),
        ],
        compiler_params=pltpu.CompilerParams(
            collective_id=0, has_side_effects=True, vmem_limit_bytes=48 * 2**20
        ),
    )(forcing.reshape(vectors * cells, LANES), vel_axial, vel_radial, coupling, viscosity)
    return basis.reshape(forcing.shape), upper


def solution(mesh):
    return jax.shard_map(
        per_device,
        mesh=mesh,
        in_specs=(
            P(None, None, "ax", "rad"),
            P("ax", "rad"),
            P("ax", "rad"),
            P(None, None, "ax", "rad"),
            P(),
        ),
        out_specs=(P(None, None, "ax", "rad"), P()),
        check_vma=False,
    )
```

```python
import functools

import jax
import jax.numpy as jnp
from jax import lax
from jax.experimental import pallas as pl
from jax.experimental.pallas import tpu as pltpu
from jax.sharding import PartitionSpec as P

STEPS = 3
time_step = 0.8

LANES = 128
SUB = 8
MESH = pl.DeviceIdType.MESH


def kernel(
    sizes, f_ref, va_ref, vr_ref, cp_ref, nu_ref, split_out, folded_ref,
    forcing_in, va_in, vr_in, cp_in, nu_in, in_sem,
    field_0, field_1, coef, packed, from_left, from_right, split, split_sem, mine, rad_slots, ax_slots,
    send_sem, recv_sem, rad_send, rad_recv, ax_send, ax_recv,
):
    vectors, variables, rows, n_ax, n_rad = sizes
    groups = vectors // SUB
    cells = variables * rows
    fields = (field_0, field_1)
    ax = lax.axis_index("ax")
    rad = lax.axis_index("rad")
    ax_before = lax.rem(ax + n_ax - 1, n_ax)
    ax_after = lax.rem(ax + 1, n_ax)
    rad_before = lax.rem(rad + n_rad - 1, n_rad)
    rad_after = lax.rem(rad + 1, n_rad)
    sends = (ax > 0, ax < n_ax - 1, rad > 0, rad < n_rad - 1)
    takes = (ax < n_ax - 1, ax > 0, rad < n_rad - 1, rad > 0)
    lane = lax.broadcasted_iota(jnp.int32, (SUB, LANES), 1)
    sub = lax.broadcasted_iota(jnp.int32, (SUB, LANES), 0)
    slot = lane // 8
    tile = (SUB, LANES)

    def link(buf, g, d):
        if d == 0:
            src, dst = fields[buf].at[g, :, 2:4], fields[buf].at[g, :, rows + 2 : rows + 4]
            device = (ax_before, rad)
        elif d == 1:
            src, dst = fields[buf].at[g, :, rows : rows + 2], fields[buf].at[g, :, 0:2]
            device = (ax_after, rad)
        elif d == 2:
            src, dst = packed.at[buf, g], from_right.at[buf, g]
            device = (ax, rad_before)
        else:
            src, dst = packed.at[buf, g], from_left.at[buf, g]
            device = (ax, rad_after)
        return pltpu.make_async_remote_copy(
            src_ref=src, dst_ref=dst,
            send_sem=send_sem.at[buf, g, d], recv_sem=recv_sem.at[buf, g, d],
            device_id=device, device_id_type=MESH,
        )

    def start(buf, g, d):
        @pl.when(sends[d])
        def _():
            link(buf, g, d).start()

    def wait_send(buf, g, d):
        @pl.when(sends[d])
        def _():
            link(buf, g, d).wait_send()

    def wait_recv(buf, g, d):
        @pl.when(takes[d])
        def _():
            link(buf, g, d).wait_recv()

    part = SUB * cells
    pieces = [
        pltpu.make_async_copy(
            f_ref.at[pl.ds(g * part, part)], forcing_in.at[pl.ds(g * part, part)], in_sem.at[g]
        )
        for g in range(groups)
    ]
    others = [
        pltpu.make_async_copy(source, target, in_sem.at[groups + i])
        for i, (source, target) in enumerate(
            ((va_ref, va_in), (vr_ref, vr_in), (cp_ref, cp_in), (nu_ref, nu_in))
        )
    ]
    for copy in pieces + others:
        copy.start()

    zero_rows = jnp.zeros((variables, 2, SUB, LANES), jnp.float32)
    zero_side = jnp.zeros((variables, SUB, LANES), jnp.float32)
    for buf in range(2):
        for g in range(groups):
            fields[buf][g, :, 0:2] = zero_rows
            fields[buf][g, :, rows + 2 : rows + 4] = zero_rows
            from_left[buf, g] = zero_side
            from_right[buf, g] = zero_side

    barrier = pltpu.get_barrier_semaphore()
    for step in range(1, n_ax):
        pl.semaphore_signal(
            barrier, inc=1, device_id=(lax.rem(ax + step, n_ax), rad), device_id_type=MESH
        )
    for step in range(1, n_rad):
        pl.semaphore_signal(
            barrier, inc=1, device_id=(ax, lax.rem(rad + step, n_rad)), device_id_type=MESH
        )

    for g in range(groups):
        pieces[g].wait()
        for v in range(variables):
            pack = jnp.zeros(tile, jnp.float32)
            for a in range(rows):
                value = forcing_in[pl.ds(g * part + v * rows + a, SUB, stride=cells), :]
                field_0[g, v, a + 2] = value
                pack = jnp.where(slot == a, pltpu.roll(value, 2 + 8 * a, 1), pack)
            packed[0, g, v] = pack
        if g == 0:
            pl.semaphore_wait(barrier, n_ax + n_rad - 2)
        for d in range(4):
            start(0, g, d)
    for copy in others:
        copy.wait()

    def prepare(a, carry):
        vel_a = jnp.broadcast_to(va_in[pl.ds(a, 1), :], tile) * (time_step / 12.0)
        vel_r = jnp.broadcast_to(vr_in[pl.ds(a, 1), :], tile) * (time_step / 12.0)
        for v in range(variables):
            nu = jnp.full(tile, nu_in[v], jnp.float32) * (time_step / 12.0)
            terms = []
            for vel in (vel_a, vel_r):
                terms += [16.0 * nu - 8.0 * vel, 16.0 * nu + 8.0 * vel, vel - nu, -vel - nu]
            for w in range(variables):
                term = time_step * jnp.broadcast_to(cp_in[v, w, pl.ds(a, 1), :], tile)
                if w == v:
                    term = term + (1.0 - 60.0 * nu)
                terms.append(term)
            for t, term in enumerate(terms):
                coef[v, a, t] = term
        return carry

    lax.fori_loop(0, rows, prepare, 0)

    def advance(src, g, start_axial):
        dst = 1 - src
        now, later = fields[src], fields[dst]
        held = []

        def store(keep):
            while len(held) > keep:
                v, a, value = held.pop(0)
                later[g, v, a + 2] = value

        sides = [
            jnp.where(lane % 8 < 2, from_left[src, g, v], from_right[src, g, v])
            for v in range(variables)
        ]
        packs = [jnp.zeros(tile, jnp.float32) for _ in range(variables)]
        order = [0, 1, rows - 2, rows - 1] + list(range(2, rows - 2))
        for count, a in enumerate(order):
            centre = [now[g, v, a + 2] for v in range(variables)]
            for v in range(variables):
                x = centre[v]
                side = pltpu.roll(sides[v], (2 * LANES - 2 - 8 * a) % LANES, 1)
                near = [
                    now[g, v, a + 3],
                    now[g, v, a + 1],
                    now[g, v, a + 4],
                    now[g, v, a],
                    pltpu.roll(jnp.where(lane == 0, side, x), LANES - 1, 1),
                    pltpu.roll(jnp.where(lane == LANES - 1, side, x), 1, 1),
                    pltpu.roll(jnp.where(lane < 2, side, x), LANES - 2, 1),
                    pltpu.roll(jnp.where(lane >= LANES - 2, side, x), 2, 1),
                ]
                parts = [coef[v, a, t] * q for t, q in enumerate(near + centre)]
                while len(parts) > 1:
                    parts = [
                        parts[i] + parts[i + 1] if i + 1 < len(parts) else parts[i]
                        for i in range(0, len(parts), 2)
                    ]
                new = parts[0]
                if src == 1:
                    new = 0.5 * (later[g, v, a + 2] + new)
                held.append((v, a, new))
                packs[v] = jnp.where(slot == a, pltpu.roll(new, 2 + 8 * a, 1), packs[v])
            if count == 3:
                store(0)
                start_axial()
            store(2 * variables)
        store(0)
        for v in range(variables):
            packed[dst, g, v] = packs[v]

    def both_halves(step, carry):
        def half(src):
            more = jnp.logical_or(step < STEPS - 1, src == 0)

            def one_group(g, inner):
                for d in range(4):
                    wait_recv(src, g, d)
                for d in range(4):
                    wait_send(src, g, d)

                def send(directions):
                    @pl.when(more)
                    def _():
                        for d in directions:
                            start(1 - src, g, d)

                advance(src, g, lambda: send((0, 1)))
                send((2, 3))
                return inner

            lax.fori_loop(0, groups, one_group, 0)

        half(0)
        half(1)
        return carry

    lax.fori_loop(0, STEPS, both_halves, 0)

    def leave(v):
        return pltpu.make_async_copy(split.at[v], split_out.at[v], split_sem.at[v])

    def products(v, total):
        for p in range(rows // 2):
            for e in range(2):
                x = jnp.concatenate(
                    [field_0[g, v, 2 * p + e + 2] for g in range(groups)], axis=0
                )
                high = x.astype(jnp.bfloat16)
                low = (x - high.astype(jnp.float32)).astype(jnp.bfloat16)
                split[v, p, :, e * LANES : (e + 1) * LANES] = jnp.concatenate(
                    [high, low, high, low], axis=0
                )
            both = split[v, p]
            total = total + lax.dot_general(
                both[: 2 * vectors], both, (((1,), (1,)), ((), ())),
                preferred_element_type=jnp.float32,
            )
        leave(v).start()
        return total

    total = lax.fori_loop(
        0, variables, products, jnp.zeros((2 * vectors, LANES), jnp.float32)
    )
    half_sum = total[:vectors] + total[vectors:]
    gram = half_sum + pltpu.roll(half_sum, vectors, 1)
    gram = gram * (1.0 / (cells * LANES * n_ax * n_rad))
    quarter = lane // vectors
    folded = gram[:SUB]
    for i in range(1, vectors // SUB):
        folded = jnp.where(quarter == i, gram[SUB * i : SUB * (i + 1)], folded)

    def sum_over(value, n, me, place, slots, sends_on, takes_on, held):
        held[...] = value
        copies = []
        for step in range(1, n):
            copy = pltpu.make_async_remote_copy(
                src_ref=held, dst_ref=slots.at[me],
                send_sem=sends_on.at[step], recv_sem=takes_on.at[step],
                device_id=place(lax.rem(me + step, n)), device_id_type=MESH,
            )
            copy.start()
            copies.append(copy)
        slots[me] = value
        for copy in copies:
            copy.wait_send()
            copy.wait_recv()
        result = slots[0]
        for i in range(1, n):
            result = result + slots[i]
        return result

    folded = sum_over(
        folded, n_rad, rad, lambda i: (ax, i), rad_slots, rad_send, rad_recv, mine.at[0]
    )
    folded = sum_over(
        folded, n_ax, ax, lambda i: (i, rad), ax_slots, ax_send, ax_recv, mine.at[1]
    )

    folded_ref[...] = folded
    for v in range(variables):
        leave(v).wait()


def finish(sizes, folded_ref, split_in, out_ref, r_ref, split, basis, in_sem, out_sem):
    vectors, variables, rows, n_ax, n_rad = sizes
    lane = lax.broadcasted_iota(jnp.int32, (SUB, LANES), 1)
    sub = lax.broadcasted_iota(jnp.int32, (SUB, LANES), 0)
    quarter = lane // vectors
    tile = (SUB, LANES)
    folded = folded_ref[...]

    def enter(v):
        return pltpu.make_async_copy(split_in.at[v], split.at[v], in_sem.at[v])

    for v in range(variables):
        enter(v).start()

    blocks = []
    for b in range(vectors // SUB):
        part = folded if b == 0 else pltpu.roll(folded, LANES - vectors * b, 1)
        unit = jnp.where(lane - vectors == sub + SUB * b, 1.0, 0.0)
        blocks.append(jnp.where(lane < vectors, part, unit))
    for j in range(vectors):
        jb, js = j // SUB, j % SUB
        row = jnp.broadcast_to(blocks[jb][js : js + 1, :], tile)
        columns = {
            b: jnp.broadcast_to(blocks[b][:, j : j + 1], tile) for b in range(jb, len(blocks))
        }
        pivot = jnp.broadcast_to(columns[jb][js : js + 1, :], tile)
        scaled = row * (1.0 / pivot)
        for b in range(jb, len(blocks)):
            change = columns[b] * scaled
            if b == jb:
                change = jnp.where(sub > js, change, 0.0)
            blocks[b] = blocks[b] - change
    lefts, rights = [], []
    for b, block in enumerate(blocks):
        diagonal = jnp.sum(
            jnp.where(lane == sub + SUB * b, block, 0.0), axis=1, keepdims=True
        )
        block = block * (1.0 / jnp.sqrt(jnp.broadcast_to(diagonal, tile)))
        lefts.append(jnp.where(lane >= sub + SUB * b, block, 0.0))
        inverse = jnp.where(quarter == 1, block, 0.0)
        inverse = inverse + pltpu.roll(inverse, vectors, 1)
        inverse = inverse + pltpu.roll(inverse, 2 * vectors, 1)
        rights.append(inverse)
    r_ref[...] = jnp.concatenate(lefts, axis=0)[:, :vectors]
    inverse = jnp.concatenate(rights, axis=0)
    high = inverse.astype(jnp.bfloat16).astype(jnp.float32)
    wide = lax.broadcasted_iota(jnp.int32, (vectors, LANES), 1)
    factors = jnp.where(wide < 2 * vectors, high, inverse - high).astype(jnp.bfloat16)

    def leave(v):
        return pltpu.make_async_copy(
            basis.at[:, v], out_ref.at[:, v], out_sem.at[v]
        )

    for v in range(variables):
        enter(v).wait()
        for p in range(rows // 2):
            found = jnp.dot(factors, split[v, p], preferred_element_type=jnp.float32)
            for e in range(2):
                basis[:, v, 2 * p + e, :] = found[:, e * LANES : (e + 1) * LANES]
        leave(v).start()
    for v in range(variables):
        leave(v).wait()


def per_device(forcing, vel_axial, vel_radial, coupling, viscosity):
    vectors, variables, rows, columns = forcing.shape
    n_ax, n_rad = lax.axis_size("ax"), lax.axis_size("rad")
    groups = vectors // SUB
    cells = variables * rows
    assert columns == LANES and rows * 8 == LANES and vectors * 4 == LANES
    f32 = jnp.float32
    vmem = pl.BlockSpec(memory_space=pltpu.VMEM)
    side = pltpu.VMEM((2, groups, variables, SUB, LANES), f32)
    field = pltpu.VMEM((groups, variables, rows + 4, SUB, LANES), f32)
    dma = pltpu.SemaphoreType.DMA
    sizes = (vectors, variables, rows, n_ax, n_rad)
    hbm = pl.BlockSpec(memory_space=pltpu.HBM)
    split, folded = pl.pallas_call(
        functools.partial(kernel, sizes),
        out_shape=(
            jax.ShapeDtypeStruct((variables, rows // 2, LANES, 2 * LANES), jnp.bfloat16),
            jax.ShapeDtypeStruct((SUB, LANES), f32),
        ),
        in_specs=[hbm] * 5,
        out_specs=(hbm, vmem),
        scratch_shapes=[
            pltpu.VMEM((vectors * cells, LANES), f32),
            pltpu.VMEM((rows, LANES), f32),
            pltpu.VMEM((rows, LANES), f32),
            pltpu.VMEM((variables, variables, rows, LANES), f32),
            pltpu.SMEM((variables,), f32),
            dma((groups + 4,)),
            field, field,
            pltpu.VMEM((variables, rows, 8 + variables, SUB, LANES), f32),
            side, side, side,
            pltpu.VMEM((variables, rows // 2, LANES, 2 * LANES), jnp.bfloat16),
            dma((variables,)),
            pltpu.VMEM((2, SUB, LANES), f32),
            pltpu.VMEM((n_rad, SUB, LANES), f32),
            pltpu.VMEM((n_ax, SUB, LANES), f32),
            dma((2, groups, 4)), dma((2, groups, 4)),
            dma((n_rad,)), dma((n_rad,)), dma((n_ax,)), dma((n_ax,)),
        ],
        compiler_params=pltpu.CompilerParams(
            collective_id=0, has_side_effects=True, vmem_limit_bytes=64 * 2**20
        ),
    )(forcing.reshape(vectors * cells, LANES), vel_axial, vel_radial, coupling, viscosity)
    return pl.pallas_call(
        functools.partial(finish, sizes),
        out_shape=(
            jax.ShapeDtypeStruct(forcing.shape, f32),
            jax.ShapeDtypeStruct((vectors, vectors), f32),
        ),
        in_specs=[vmem, hbm],
        out_specs=(hbm, vmem),
        scratch_shapes=[
            pltpu.VMEM(split.shape, split.dtype),
            pltpu.VMEM(forcing.shape, f32),
            dma((variables,)), dma((variables,)),
        ],
        compiler_params=pltpu.CompilerParams(vmem_limit_bytes=64 * 2**20),
    )(folded, split)


def solution(mesh):
    return jax.shard_map(
        per_device,
        mesh=mesh,
        in_specs=(
            P(None, None, "ax", "rad"),
            P("ax", "rad"),
            P("ax", "rad"),
            P(None, None, "ax", "rad"),
            P(),
        ),
        out_specs=(P(None, None, "ax", "rad"), P()),
        check_vma=False,
    )
```

```python
import functools

import jax
import jax.numpy as jnp
from jax import lax
from jax.experimental import pallas as pl
from jax.experimental.pallas import tpu as pltpu
from jax.sharding import PartitionSpec as P

STEPS = 3
time_step = 0.8

LANES = 128
SUB = 8
MESH = pl.DeviceIdType.MESH


def kernel(
    sizes, f_ref, va_ref, vr_ref, cp_ref, nu_ref, split_out, folded_ref,
    forcing_in, va_in, vr_in, cp_in, nu_in, in_sem,
    field_0, field_1, coef, packed, from_left, from_right, split, split_sem, mine, rad_slots, ax_slots,
    send_sem, recv_sem, rad_send, rad_recv, ax_send, ax_recv,
):
    vectors, variables, rows, n_ax, n_rad = sizes
    groups = vectors // SUB
    cells = variables * rows
    fields = (field_0, field_1)
    ax = lax.axis_index("ax")
    rad = lax.axis_index("rad")
    ax_before = lax.rem(ax + n_ax - 1, n_ax)
    ax_after = lax.rem(ax + 1, n_ax)
    rad_before = lax.rem(rad + n_rad - 1, n_rad)
    rad_after = lax.rem(rad + 1, n_rad)
    sends = (ax > 0, ax < n_ax - 1, rad > 0, rad < n_rad - 1)
    takes = (ax < n_ax - 1, ax > 0, rad < n_rad - 1, rad > 0)
    lane = lax.broadcasted_iota(jnp.int32, (SUB, LANES), 1)
    sub = lax.broadcasted_iota(jnp.int32, (SUB, LANES), 0)
    slot = lane // 8
    tile = (SUB, LANES)

    def link(buf, g, d):
        if d == 0:
            src, dst = fields[buf].at[g, :, 2:4], fields[buf].at[g, :, rows + 2 : rows + 4]
            device = (ax_before, rad)
        elif d == 1:
            src, dst = fields[buf].at[g, :, rows : rows + 2], fields[buf].at[g, :, 0:2]
            device = (ax_after, rad)
        elif d == 2:
            src, dst = packed.at[buf, g], from_right.at[buf, g]
            device = (ax, rad_before)
        else:
            src, dst = packed.at[buf, g], from_left.at[buf, g]
            device = (ax, rad_after)
        return pltpu.make_async_remote_copy(
            src_ref=src, dst_ref=dst,
            send_sem=send_sem.at[buf, g, d], recv_sem=recv_sem.at[buf, g, d],
            device_id=device, device_id_type=MESH,
        )

    def start(buf, g, d):
        @pl.when(sends[d])
        def _():
            link(buf, g, d).start()

    def wait_send(buf, g, d):
        @pl.when(sends[d])
        def _():
            link(buf, g, d).wait_send()

    def wait_recv(buf, g, d):
        @pl.when(takes[d])
        def _():
            link(buf, g, d).wait_recv()

    part = SUB * cells
    pieces = [
        pltpu.make_async_copy(
            f_ref.at[pl.ds(g * part, part)], forcing_in.at[pl.ds(g * part, part)], in_sem.at[g]
        )
        for g in range(groups)
    ]
    others = [
        pltpu.make_async_copy(source, target, in_sem.at[groups + i])
        for i, (source, target) in enumerate(
            ((va_ref, va_in), (vr_ref, vr_in), (cp_ref, cp_in), (nu_ref, nu_in))
        )
    ]
    for copy in pieces + others:
        copy.start()

    zero_rows = jnp.zeros((variables, 2, SUB, LANES), jnp.float32)
    zero_side = jnp.zeros((variables, SUB, LANES), jnp.float32)
    for buf in range(2):
        for g in range(groups):
            fields[buf][g, :, 0:2] = zero_rows
            fields[buf][g, :, rows + 2 : rows + 4] = zero_rows
            from_left[buf, g] = zero_side
            from_right[buf, g] = zero_side

    barrier = pltpu.get_barrier_semaphore()
    for step in range(1, n_ax):
        pl.semaphore_signal(
            barrier, inc=1, device_id=(lax.rem(ax + step, n_ax), rad), device_id_type=MESH
        )
    for step in range(1, n_rad):
        pl.semaphore_signal(
            barrier, inc=1, device_id=(ax, lax.rem(rad + step, n_rad)), device_id_type=MESH
        )

    for g in range(groups):
        pieces[g].wait()
        for v in range(variables):
            pack = jnp.zeros(tile, jnp.float32)
            for a in range(rows):
                value = forcing_in[pl.ds(g * part + v * rows + a, SUB, stride=cells), :]
                field_0[g, v, a + 2] = value
                pack = jnp.where(slot == a, pltpu.roll(value, 2 + 8 * a, 1), pack)
            packed[0, g, v] = pack
        if g == 0:
            pl.semaphore_wait(barrier, n_ax + n_rad - 2)
        for d in range(4):
            start(0, g, d)
    for copy in others:
        copy.wait()

    def prepare(a, carry):
        vel_a = jnp.broadcast_to(va_in[pl.ds(a, 1), :], tile) * (time_step / 12.0)
        vel_r = jnp.broadcast_to(vr_in[pl.ds(a, 1), :], tile) * (time_step / 12.0)
        for v in range(variables):
            nu = jnp.full(tile, nu_in[v], jnp.float32) * (time_step / 12.0)
            terms = []
            for vel in (vel_a, vel_r):
                terms += [16.0 * nu - 8.0 * vel, 16.0 * nu + 8.0 * vel, vel - nu, -vel - nu]
            for w in range(variables):
                term = time_step * jnp.broadcast_to(cp_in[v, w, pl.ds(a, 1), :], tile)
                if w == v:
                    term = term + (1.0 - 60.0 * nu)
                terms.append(term)
            for t, term in enumerate(terms):
                coef[v, a, t] = term
        return carry

    lax.fori_loop(0, rows, prepare, 0)

    def advance(src, g, start_axial):
        dst = 1 - src
        now, later = fields[src], fields[dst]
        held = []

        def store(keep):
            while len(held) > keep:
                v, a, value = held.pop(0)
                later[g, v, a + 2] = value

        sides = [
            jnp.where(lane % 8 < 2, from_left[src, g, v], from_right[src, g, v])
            for v in range(variables)
        ]
        packs = [jnp.zeros(tile, jnp.float32) for _ in range(variables)]
        order = [0, 1, rows - 2, rows - 1] + list(range(2, rows - 2))
        for count, a in enumerate(order):
            centre = [now[g, v, a + 2] for v in range(variables)]
            for v in range(variables):
                x = centre[v]
                side = pltpu.roll(sides[v], (2 * LANES - 2 - 8 * a) % LANES, 1)
                near = [
                    now[g, v, a + 3],
                    now[g, v, a + 1],
                    now[g, v, a + 4],
                    now[g, v, a],
                    pltpu.roll(jnp.where(lane == 0, side, x), LANES - 1, 1),
                    pltpu.roll(jnp.where(lane == LANES - 1, side, x), 1, 1),
                    pltpu.roll(jnp.where(lane < 2, side, x), LANES - 2, 1),
                    pltpu.roll(jnp.where(lane >= LANES - 2, side, x), 2, 1),
                ]
                parts = [coef[v, a, t] * q for t, q in enumerate(near + centre)]
                while len(parts) > 1:
                    parts = [
                        parts[i] + parts[i + 1] if i + 1 < len(parts) else parts[i]
                        for i in range(0, len(parts), 2)
                    ]
                new = parts[0]
                if src == 1:
                    new = 0.5 * (later[g, v, a + 2] + new)
                held.append((v, a, new))
                packs[v] = jnp.where(slot == a, pltpu.roll(new, 2 + 8 * a, 1), packs[v])
            if count == 3:
                store(0)
                start_axial()
            store(2 * variables)
        store(0)
        for v in range(variables):
            packed[dst, g, v] = packs[v]

    def both_halves(step, carry):
        def half(src):
            more = jnp.logical_or(step < STEPS - 1, src == 0)

            def one_group(g, inner):
                for d in range(4):
                    wait_recv(src, g, d)
                if src == 1:
                    for d in range(4):
                        wait_send(0, g, d)
                else:
                    @pl.when(step > 0)
                    def _():
                        for d in range(4):
                            wait_send(1, g, d)


                def send(directions):
                    @pl.when(more)
                    def _():
                        for d in directions:
                            start(1 - src, g, d)

                advance(src, g, lambda: send((0, 1)))
                send((2, 3))
                return inner

            lax.fori_loop(0, groups, one_group, 0)

        half(0)
        half(1)
        return carry

    lax.fori_loop(0, STEPS, both_halves, 0)

    def drain(g, carry):
        for d in range(4):
            wait_send(1, g, d)
        return carry

    lax.fori_loop(0, groups, drain, 0)

    def leave(v):
        return pltpu.make_async_copy(split.at[v], split_out.at[v], split_sem.at[v])

    def products(v, total):
        for p in range(rows // 2):
            for e in range(2):
                x = jnp.concatenate(
                    [field_0[g, v, 2 * p + e + 2] for g in range(groups)], axis=0
                )
                high = x.astype(jnp.bfloat16)
                low = (x - high.astype(jnp.float32)).astype(jnp.bfloat16)
                split[v, p, :, e * LANES : (e + 1) * LANES] = jnp.concatenate(
                    [high, low, high, low], axis=0
                )
            both = split[v, p]
            total = total + lax.dot_general(
                both[: 2 * vectors], both, (((1,), (1,)), ((), ())),
                preferred_element_type=jnp.float32,
            )
        leave(v).start()
        return total

    total = lax.fori_loop(
        0, variables, products, jnp.zeros((2 * vectors, LANES), jnp.float32)
    )
    half_sum = total[:vectors] + total[vectors:]
    gram = half_sum + pltpu.roll(half_sum, vectors, 1)
    gram = gram * (1.0 / (cells * LANES * n_ax * n_rad))
    quarter = lane // vectors
    folded = gram[:SUB]
    for i in range(1, vectors // SUB):
        folded = jnp.where(quarter == i, gram[SUB * i : SUB * (i + 1)], folded)

    def sum_over(value, n, me, place, slots, sends_on, takes_on, held):
        held[...] = value
        copies = []
        for step in range(1, n):
            copy = pltpu.make_async_remote_copy(
                src_ref=held, dst_ref=slots.at[me],
                send_sem=sends_on.at[step], recv_sem=takes_on.at[step],
                device_id=place(lax.rem(me + step, n)), device_id_type=MESH,
            )
            copy.start()
            copies.append(copy)
        slots[me] = value
        for copy in copies:
            copy.wait_send()
            copy.wait_recv()
        result = slots[0]
        for i in range(1, n):
            result = result + slots[i]
        return result

    folded = sum_over(
        folded, n_rad, rad, lambda i: (ax, i), rad_slots, rad_send, rad_recv, mine.at[0]
    )
    folded = sum_over(
        folded, n_ax, ax, lambda i: (i, rad), ax_slots, ax_send, ax_recv, mine.at[1]
    )

    folded_ref[...] = folded
    for v in range(variables):
        leave(v).wait()


def finish(sizes, folded_ref, split_in, out_ref, r_ref, split, basis, in_sem, out_sem):
    vectors, variables, rows, n_ax, n_rad = sizes
    lane = lax.broadcasted_iota(jnp.int32, (SUB, LANES), 1)
    sub = lax.broadcasted_iota(jnp.int32, (SUB, LANES), 0)
    quarter = lane // vectors
    tile = (SUB, LANES)
    folded = folded_ref[...]

    def enter(v):
        return pltpu.make_async_copy(split_in.at[v], split.at[v], in_sem.at[v])

    for v in range(variables):
        enter(v).start()

    blocks = []
    for b in range(vectors // SUB):
        part = folded if b == 0 else pltpu.roll(folded, LANES - vectors * b, 1)
        unit = jnp.where(lane - vectors == sub + SUB * b, 1.0, 0.0)
        blocks.append(jnp.where(lane < vectors, part, unit))
    for j in range(0, vectors, 2):
        jb, js = j // SUB, j % SUB
        below = range(jb, len(blocks))
        first = jnp.broadcast_to(blocks[jb][js : js + 1, :], tile)
        second = jnp.broadcast_to(blocks[jb][js + 1 : js + 2, :], tile)
        column = {b: jnp.broadcast_to(blocks[b][:, j : j + 1], tile) for b in below}
        other = {b: jnp.broadcast_to(blocks[b][:, j + 1 : j + 2], tile) for b in below}

        def entry(columns, i):
            return jnp.broadcast_to(columns[jb][i : i + 1, :], tile)

        over = 1.0 / entry(column, js)
        ratio = entry(column, js + 1) * over
        across = entry(other, js) * over
        last = 1.0 / (entry(other, js + 1) - ratio * entry(other, js))
        first_scaled = first * over
        second_scaled = (second - ratio * first) * last
        for b in below:
            change = column[b] * first_scaled
            more = (other[b] - column[b] * across) * second_scaled
            if b == jb:
                change = jnp.where(sub > js, change, 0.0)
                more = jnp.where(sub > js + 1, more, 0.0)
            blocks[b] = blocks[b] - change - more
    lefts, rights = [], []
    for b, block in enumerate(blocks):
        diagonal = jnp.sum(
            jnp.where(lane == sub + SUB * b, block, 0.0), axis=1, keepdims=True
        )
        block = block * (1.0 / jnp.sqrt(jnp.broadcast_to(diagonal, tile)))
        lefts.append(jnp.where(lane >= sub + SUB * b, block, 0.0))
        inverse = jnp.where(quarter == 1, block, 0.0)
        inverse = inverse + pltpu.roll(inverse, vectors, 1)
        inverse = inverse + pltpu.roll(inverse, 2 * vectors, 1)
        rights.append(inverse)
    r_ref[...] = jnp.concatenate(lefts, axis=0)[:, :vectors]
    inverse = jnp.concatenate(rights, axis=0)
    high = inverse.astype(jnp.bfloat16).astype(jnp.float32)
    wide = lax.broadcasted_iota(jnp.int32, (vectors, LANES), 1)
    factors = jnp.where(wide < 2 * vectors, high, inverse - high).astype(jnp.bfloat16)

    def leave(v):
        return pltpu.make_async_copy(
            basis.at[:, v], out_ref.at[:, v], out_sem.at[v]
        )

    for v in range(variables):
        enter(v).wait()
        for p in range(rows // 2):
            found = jnp.dot(factors, split[v, p], preferred_element_type=jnp.float32)
            for e in range(2):
                basis[:, v, 2 * p + e, :] = found[:, e * LANES : (e + 1) * LANES]
        leave(v).start()
    for v in range(variables):
        leave(v).wait()


def per_device(forcing, vel_axial, vel_radial, coupling, viscosity):
    vectors, variables, rows, columns = forcing.shape
    n_ax, n_rad = lax.axis_size("ax"), lax.axis_size("rad")
    groups = vectors // SUB
    cells = variables * rows
    assert columns == LANES and rows * 8 == LANES and vectors * 4 == LANES
    f32 = jnp.float32
    vmem = pl.BlockSpec(memory_space=pltpu.VMEM)
    side = pltpu.VMEM((2, groups, variables, SUB, LANES), f32)
    field = pltpu.VMEM((groups, variables, rows + 4, SUB, LANES), f32)
    dma = pltpu.SemaphoreType.DMA
    sizes = (vectors, variables, rows, n_ax, n_rad)
    hbm = pl.BlockSpec(memory_space=pltpu.HBM)
    split, folded = pl.pallas_call(
        functools.partial(kernel, sizes),
        out_shape=(
            jax.ShapeDtypeStruct((variables, rows // 2, LANES, 2 * LANES), jnp.bfloat16),
            jax.ShapeDtypeStruct((SUB, LANES), f32),
        ),
        in_specs=[hbm] * 5,
        out_specs=(hbm, vmem),
        scratch_shapes=[
            pltpu.VMEM((vectors * cells, LANES), f32),
            pltpu.VMEM((rows, LANES), f32),
            pltpu.VMEM((rows, LANES), f32),
            pltpu.VMEM((variables, variables, rows, LANES), f32),
            pltpu.SMEM((variables,), f32),
            dma((groups + 4,)),
            field, field,
            pltpu.VMEM((variables, rows, 8 + variables, SUB, LANES), f32),
            side, side, side,
            pltpu.VMEM((variables, rows // 2, LANES, 2 * LANES), jnp.bfloat16),
            dma((variables,)),
            pltpu.VMEM((2, SUB, LANES), f32),
            pltpu.VMEM((n_rad, SUB, LANES), f32),
            pltpu.VMEM((n_ax, SUB, LANES), f32),
            dma((2, groups, 4)), dma((2, groups, 4)),
            dma((n_rad,)), dma((n_rad,)), dma((n_ax,)), dma((n_ax,)),
        ],
        compiler_params=pltpu.CompilerParams(
            collective_id=0, has_side_effects=True, vmem_limit_bytes=64 * 2**20
        ),
    )(forcing.reshape(vectors * cells, LANES), vel_axial, vel_radial, coupling, viscosity)
    return pl.pallas_call(
        functools.partial(finish, sizes),
        out_shape=(
            jax.ShapeDtypeStruct(forcing.shape, f32),
            jax.ShapeDtypeStruct((vectors, vectors), f32),
        ),
        in_specs=[vmem, hbm],
        out_specs=(hbm, vmem),
        scratch_shapes=[
            pltpu.VMEM(split.shape, split.dtype),
            pltpu.VMEM(forcing.shape, f32),
            dma((variables,)), dma((variables,)),
        ],
        compiler_params=pltpu.CompilerParams(vmem_limit_bytes=64 * 2**20),
    )(folded, split)


def solution(mesh):
    return jax.shard_map(
        per_device,
        mesh=mesh,
        in_specs=(
            P(None, None, "ax", "rad"),
            P("ax", "rad"),
            P("ax", "rad"),
            P(None, None, "ax", "rad"),
            P(),
        ),
        out_specs=(P(None, None, "ax", "rad"), P()),
        check_vma=False,
    )
```

```python
import functools

import jax
import jax.numpy as jnp
from jax import lax
from jax.experimental import pallas as pl
from jax.experimental.pallas import tpu as pltpu
from jax.sharding import PartitionSpec as P

STEPS = 3
time_step = 0.8

LANES = 128
SUB = 8
MESH = pl.DeviceIdType.MESH


def kernel(
    sizes, f_ref, va_ref, vr_ref, cp_ref, nu_ref, split_out, folded_ref,
    forcing_in, va_in, vr_in, cp_in, nu_in, in_sem, swap_send, swap_recv,
    response, back_own, back_send, back_recv,
    field_0, field_1, coef, packed, from_left, from_right, split, split_sem, mine, rad_slots, ax_slots,
    send_sem, recv_sem, rad_send, rad_recv, ax_send, ax_recv,
):
    vectors, variables, own_rows, n_ax, n_rad = sizes
    rows = 2 * own_rows
    groups = vectors // SUB // 2
    cells = variables * own_rows
    pieces_a_side = rows * 8 // LANES
    fields = (field_0, field_1)
    ax = lax.axis_index("ax")
    rad = lax.axis_index("rad")
    ax_before = lax.rem(ax + n_ax - 2, n_ax)
    ax_after = lax.rem(ax + 2, n_ax)
    half_index = lax.rem(ax, 2)
    partner = ax + 1 - 2 * half_index
    rad_before = lax.rem(rad + n_rad - 1, n_rad)
    rad_after = lax.rem(rad + 1, n_rad)
    sends = (ax > 1, ax < n_ax - 2, rad > 0, rad < n_rad - 1)
    takes = (ax < n_ax - 2, ax > 1, rad < n_rad - 1, rad > 0)
    lane = lax.broadcasted_iota(jnp.int32, (SUB, LANES), 1)
    sub = lax.broadcasted_iota(jnp.int32, (SUB, LANES), 0)
    slot = lane // 8
    tile = (SUB, LANES)

    def link(buf, g, d):
        if d == 0:
            src, dst = fields[buf].at[g, :, 2:4], fields[buf].at[g, :, rows + 2 : rows + 4]
            device = (ax_before, rad)
        elif d == 1:
            src, dst = fields[buf].at[g, :, rows : rows + 2], fields[buf].at[g, :, 0:2]
            device = (ax_after, rad)
        elif d == 2:
            src, dst = packed.at[buf, g], from_right.at[buf, g]
            device = (ax, rad_before)
        else:
            src, dst = packed.at[buf, g], from_left.at[buf, g]
            device = (ax, rad_after)
        return pltpu.make_async_remote_copy(
            src_ref=src, dst_ref=dst,
            send_sem=send_sem.at[buf, g, d], recv_sem=recv_sem.at[buf, g, d],
            device_id=device, device_id_type=MESH,
        )

    def start(buf, g, d):
        @pl.when(sends[d])
        def _():
            link(buf, g, d).start()

    def wait_send(buf, g, d):
        @pl.when(sends[d])
        def _():
            link(buf, g, d).wait_send()

    def wait_recv(buf, g, d):
        @pl.when(takes[d])
        def _():
            link(buf, g, d).wait_recv()

    part = SUB * cells

    def enter(i):
        if i < groups:
            span = pl.ds((half_index * groups + i) * part, part)
            return f_ref.at[span], forcing_in.at[half_index, pl.ds(i * part, part)]
        source, target = ((va_ref, va_in), (vr_ref, vr_in), (cp_ref, cp_in))[i - groups]
        return source, target.at[half_index]

    def swap(i):
        source, target = enter(i)
        if i < groups:
            source = f_ref.at[pl.ds(((1 - half_index) * groups + i) * part, part)]
        return pltpu.make_async_remote_copy(
            src_ref=source, dst_ref=target,
            send_sem=swap_send.at[i], recv_sem=swap_recv.at[i],
            device_id=(partner, rad), device_id_type=MESH,
        )

    own = [pltpu.make_async_copy(*enter(i), in_sem.at[i]) for i in range(groups + 3)]
    own.append(pltpu.make_async_copy(nu_ref, nu_in, in_sem.at[groups + 3]))
    swaps = [swap(i) for i in range(groups + 3)]
    for copy in own:
        copy.start()

    zero_rows = jnp.zeros((variables, 2, SUB, LANES), jnp.float32)
    zero_side = jnp.zeros((variables, pieces_a_side, SUB, LANES), jnp.float32)
    for buf in range(2):
        for g in range(groups):
            fields[buf][g, :, 0:2] = zero_rows
            fields[buf][g, :, rows + 2 : rows + 4] = zero_rows
            from_left[buf, g] = zero_side
            from_right[buf, g] = zero_side

    barrier = pltpu.get_barrier_semaphore()
    for step in range(1, n_ax):
        pl.semaphore_signal(
            barrier, inc=1, device_id=(lax.rem(ax + step, n_ax), rad), device_id_type=MESH
        )
    for step in range(1, n_rad):
        pl.semaphore_signal(
            barrier, inc=1, device_id=(ax, lax.rem(rad + step, n_rad)), device_id_type=MESH
        )

    pl.semaphore_wait(barrier, n_ax + n_rad - 2)
    order = list(range(groups, groups + 3)) + list(range(groups))
    for i in order:
        swaps[i].start()
    own[groups + 3].wait()
    for i in range(groups, groups + 3):
        own[i].wait()
        swaps[i].wait_recv()

    def prepare(h, a, carry):
        vel_a = jnp.broadcast_to(va_in[h, pl.ds(a, 1), :], tile) * (time_step / 12.0)
        vel_r = jnp.broadcast_to(vr_in[h, pl.ds(a, 1), :], tile) * (time_step / 12.0)
        for v in range(variables):
            nu = jnp.full(tile, nu_in[v], jnp.float32) * (time_step / 12.0)
            terms = []
            for vel in (vel_a, vel_r):
                terms += [16.0 * nu - 8.0 * vel, 16.0 * nu + 8.0 * vel, vel - nu, -vel - nu]
            for w in range(variables):
                term = time_step * jnp.broadcast_to(cp_in[h, v, w, pl.ds(a, 1), :], tile)
                if w == v:
                    term = term + (1.0 - 60.0 * nu)
                terms.append(term)
            for t, term in enumerate(terms):
                coef[v, h * own_rows + a, t] = term
        return carry

    for h in range(2):
        lax.fori_loop(0, own_rows, functools.partial(prepare, h), 0)

    for g in range(groups):
        own[g].wait()
        swaps[g].wait_recv()

        def bring(v, carry):
            packs = [jnp.zeros(tile, jnp.float32) for _ in range(pieces_a_side)]
            for a in range(rows):
                start_row = g * part + v * own_rows + a % own_rows
                value = forcing_in[a // own_rows, pl.ds(start_row, SUB, stride=cells), :]
                field_0[g, v, a + 2] = value
                p, at = a * 8 // LANES, a % (LANES // 8)
                packs[p] = jnp.where(slot == at, pltpu.roll(value, 2 + 8 * at, 1), packs[p])
            for p, pack in enumerate(packs):
                packed[0, g, v, p] = pack
            return carry

        lax.fori_loop(0, variables, bring, 0)
        for d in range(4):
            start(0, g, d)
    for copy in swaps:
        copy.wait_send()

    def advance(src, g, start_axial):
        dst = 1 - src
        now, later = fields[src], fields[dst]
        held = []

        def store(keep):
            while len(held) > keep:
                v, a, value = held.pop(0)
                later[g, v, a + 2] = value

        sides = [
            [
                jnp.where(lane % 8 < 2, from_left[src, g, v, p], from_right[src, g, v, p])
                for p in range(pieces_a_side)
            ]
            for v in range(variables)
        ]
        packs = [
            [jnp.zeros(tile, jnp.float32) for _ in range(pieces_a_side)]
            for _ in range(variables)
        ]
        order = [0, 1, rows - 2, rows - 1] + list(range(2, rows - 2))
        for count, a in enumerate(order):
            p, at = a * 8 // LANES, a % (LANES // 8)
            centre = [now[g, v, a + 2] for v in range(variables)]
            for v in range(variables):
                x = centre[v]
                side = pltpu.roll(sides[v][p], (2 * LANES - 2 - 8 * at) % LANES, 1)
                near = [
                    now[g, v, a + 3],
                    now[g, v, a + 1],
                    now[g, v, a + 4],
                    now[g, v, a],
                    pltpu.roll(jnp.where(lane == 0, side, x), LANES - 1, 1),
                    pltpu.roll(jnp.where(lane == LANES - 1, side, x), 1, 1),
                    pltpu.roll(jnp.where(lane < 2, side, x), LANES - 2, 1),
                    pltpu.roll(jnp.where(lane >= LANES - 2, side, x), 2, 1),
                ]
                parts = [coef[v, a, t] * q for t, q in enumerate(near + centre)]
                while len(parts) > 1:
                    parts = [
                        parts[i] + parts[i + 1] if i + 1 < len(parts) else parts[i]
                        for i in range(0, len(parts), 2)
                    ]
                new = parts[0]
                if src == 1:
                    new = 0.5 * (later[g, v, a + 2] + new)
                held.append((v, a, new))
                packs[v][p] = jnp.where(
                    slot == at, pltpu.roll(new, 2 + 8 * at, 1), packs[v][p]
                )
            if count == 3:
                store(0)
                start_axial()
            store(2 * variables)
        store(0)
        for v in range(variables):
            for p in range(pieces_a_side):
                packed[dst, g, v, p] = packs[v][p]

    def back(g):
        return pltpu.make_async_remote_copy(
            src_ref=field_0.at[g, :, pl.ds(2 + (1 - half_index) * own_rows, own_rows)],
            dst_ref=response.at[half_index * groups + g],
            send_sem=back_send.at[g], recv_sem=back_recv.at[g],
            device_id=(partner, rad), device_id_type=MESH,
        )

    def keep(g):
        return pltpu.make_async_copy(
            field_0.at[g, :, pl.ds(2 + half_index * own_rows, own_rows)],
            response.at[half_index * groups + g], back_own.at[g],
        )

    def both_halves(step, carry):
        def half(src):
            more = jnp.logical_or(step < STEPS - 1, src == 0)

            def one_group(g, inner):
                for d in range(4):
                    wait_recv(src, g, d)
                if src == 1:
                    for d in range(4):
                        wait_send(0, g, d)
                else:
                    @pl.when(step > 0)
                    def _():
                        for d in range(4):
                            wait_send(1, g, d)


                def send(directions):
                    @pl.when(more)
                    def _():
                        for d in directions:
                            start(1 - src, g, d)

                advance(src, g, lambda: send((0, 1)))
                send((2, 3))
                if src == 1:
                    @pl.when(step == STEPS - 1)
                    def _():
                        back(g).start()
                        keep(g).start()
                return inner

            lax.fori_loop(0, groups, one_group, 0)

        half(0)
        half(1)
        return carry

    lax.fori_loop(0, STEPS, both_halves, 0)

    def drain(g, carry):
        for d in range(4):
            wait_send(1, g, d)
        return carry

    lax.fori_loop(0, groups, drain, 0)
    for g in range(groups):
        keep(g).wait()
        back(g).wait_recv()
        back(g).wait_send()

    def leave(v):
        return pltpu.make_async_copy(split.at[v], split_out.at[v], split_sem.at[v])

    def products(v, total):
        for p in range(own_rows // 2):
            for e in range(2):
                x = jnp.concatenate(
                    [response[g, v, 2 * p + e] for g in range(2 * groups)], axis=0
                )
                high = x.astype(jnp.bfloat16)
                low = (x - high.astype(jnp.float32)).astype(jnp.bfloat16)
                split[v, p, :, e * LANES : (e + 1) * LANES] = jnp.concatenate(
                    [high, low, high, low], axis=0
                )
            both = split[v, p]
            total = total + lax.dot_general(
                both[: 2 * vectors], both, (((1,), (1,)), ((), ())),
                preferred_element_type=jnp.float32,
            )
        leave(v).start()
        return total

    total = lax.fori_loop(
        0, variables, products, jnp.zeros((2 * vectors, LANES), jnp.float32)
    )
    half_sum = total[:vectors] + total[vectors:]
    gram = half_sum + pltpu.roll(half_sum, vectors, 1)
    gram = gram * (1.0 / (cells * LANES * n_ax * n_rad))
    quarter = lane // vectors
    folded = gram[:SUB]
    for i in range(1, vectors // SUB):
        folded = jnp.where(quarter == i, gram[SUB * i : SUB * (i + 1)], folded)

    def sum_over(value, n, me, place, slots, sends_on, takes_on, held):
        held[...] = value
        copies = []
        for step in range(1, n):
            copy = pltpu.make_async_remote_copy(
                src_ref=held, dst_ref=slots.at[me],
                send_sem=sends_on.at[step], recv_sem=takes_on.at[step],
                device_id=place(lax.rem(me + step, n)), device_id_type=MESH,
            )
            copy.start()
            copies.append(copy)
        slots[me] = value
        for copy in copies:
            copy.wait_send()
            copy.wait_recv()
        result = slots[0]
        for i in range(1, n):
            result = result + slots[i]
        return result

    folded = sum_over(
        folded, n_rad, rad, lambda i: (ax, i), rad_slots, rad_send, rad_recv, mine.at[0]
    )
    folded = sum_over(
        folded, n_ax, ax, lambda i: (i, rad), ax_slots, ax_send, ax_recv, mine.at[1]
    )

    folded_ref[...] = folded
    for v in range(variables):
        leave(v).wait()


def finish(sizes, folded_ref, split_in, out_ref, r_ref, split, basis, in_sem, out_sem):
    vectors, variables, rows, n_ax, n_rad = sizes
    lane = lax.broadcasted_iota(jnp.int32, (SUB, LANES), 1)
    sub = lax.broadcasted_iota(jnp.int32, (SUB, LANES), 0)
    quarter = lane // vectors
    tile = (SUB, LANES)
    folded = folded_ref[...]

    def enter(v):
        return pltpu.make_async_copy(split_in.at[v], split.at[v], in_sem.at[v])

    for v in range(variables):
        enter(v).start()

    blocks = []
    for b in range(vectors // SUB):
        part = folded if b == 0 else pltpu.roll(folded, LANES - vectors * b, 1)
        unit = jnp.where(lane - vectors == sub + SUB * b, 1.0, 0.0)
        blocks.append(jnp.where(lane < vectors, part, unit))
    for j in range(0, vectors, 2):
        jb, js = j // SUB, j % SUB
        below = range(jb, len(blocks))
        first = jnp.broadcast_to(blocks[jb][js : js + 1, :], tile)
        second = jnp.broadcast_to(blocks[jb][js + 1 : js + 2, :], tile)
        column = {b: jnp.broadcast_to(blocks[b][:, j : j + 1], tile) for b in below}
        other = {b: jnp.broadcast_to(blocks[b][:, j + 1 : j + 2], tile) for b in below}

        def entry(columns, i):
            return jnp.broadcast_to(columns[jb][i : i + 1, :], tile)

        over = 1.0 / entry(column, js)
        ratio = entry(column, js + 1) * over
        across = entry(other, js) * over
        last = 1.0 / (entry(other, js + 1) - ratio * entry(other, js))
        first_scaled = first * over
        second_scaled = (second - ratio * first) * last
        for b in below:
            change = column[b] * first_scaled
            more = (other[b] - column[b] * across) * second_scaled
            if b == jb:
                change = jnp.where(sub > js, change, 0.0)
                more = jnp.where(sub > js + 1, more, 0.0)
            blocks[b] = blocks[b] - change - more
    lefts, rights = [], []
    for b, block in enumerate(blocks):
        diagonal = jnp.sum(
            jnp.where(lane == sub + SUB * b, block, 0.0), axis=1, keepdims=True
        )
        block = block * (1.0 / jnp.sqrt(jnp.broadcast_to(diagonal, tile)))
        lefts.append(jnp.where(lane >= sub + SUB * b, block, 0.0))
        inverse = jnp.where(quarter == 1, block, 0.0)
        inverse = inverse + pltpu.roll(inverse, vectors, 1)
        inverse = inverse + pltpu.roll(inverse, 2 * vectors, 1)
        rights.append(inverse)
    r_ref[...] = jnp.concatenate(lefts, axis=0)[:, :vectors]
    inverse = jnp.concatenate(rights, axis=0)
    high = inverse.astype(jnp.bfloat16).astype(jnp.float32)
    wide = lax.broadcasted_iota(jnp.int32, (vectors, LANES), 1)
    factors = jnp.where(wide < 2 * vectors, high, inverse - high).astype(jnp.bfloat16)

    def leave(v):
        return pltpu.make_async_copy(
            basis.at[:, v], out_ref.at[:, v], out_sem.at[v]
        )

    for v in range(variables):
        enter(v).wait()
        for p in range(rows // 2):
            found = jnp.dot(factors, split[v, p], preferred_element_type=jnp.float32)
            for e in range(2):
                basis[:, v, 2 * p + e, :] = found[:, e * LANES : (e + 1) * LANES]
        leave(v).start()
    for v in range(variables):
        leave(v).wait()


def per_device(forcing, vel_axial, vel_radial, coupling, viscosity):
    vectors, variables, rows, columns = forcing.shape
    n_ax, n_rad = lax.axis_size("ax"), lax.axis_size("rad")
    groups = vectors // SUB
    half = groups // 2
    cells = variables * rows
    assert lax.axis_size("ax") % 2 == 0
    assert columns == LANES and rows * 8 == LANES and vectors * 4 == LANES
    f32 = jnp.float32
    vmem = pl.BlockSpec(memory_space=pltpu.VMEM)
    side = pltpu.VMEM((2, half, variables, 2 * rows * 8 // LANES, SUB, LANES), f32)
    field = pltpu.VMEM((half, variables, 2 * rows + 4, SUB, LANES), f32)
    dma = pltpu.SemaphoreType.DMA
    sizes = (vectors, variables, rows, n_ax, n_rad)
    hbm = pl.BlockSpec(memory_space=pltpu.HBM)
    split, folded = pl.pallas_call(
        functools.partial(kernel, sizes),
        out_shape=(
            jax.ShapeDtypeStruct((variables, rows // 2, LANES, 2 * LANES), jnp.bfloat16),
            jax.ShapeDtypeStruct((SUB, LANES), f32),
        ),
        in_specs=[hbm] * 5,
        out_specs=(hbm, vmem),
        scratch_shapes=[
            pltpu.VMEM((2, half * SUB * cells, LANES), f32),
            pltpu.VMEM((2, rows, LANES), f32),
            pltpu.VMEM((2, rows, LANES), f32),
            pltpu.VMEM((2, variables, variables, rows, LANES), f32),
            pltpu.SMEM((variables,), f32),
            dma((half + 4,)), dma((half + 3,)), dma((half + 3,)),
            pltpu.VMEM((groups, variables, rows, SUB, LANES), f32),
            dma((half,)), dma((half,)), dma((half,)),
            field, field,
            pltpu.VMEM((variables, 2 * rows, 8 + variables, SUB, LANES), f32),
            side, side, side,
            pltpu.VMEM((variables, rows // 2, LANES, 2 * LANES), jnp.bfloat16),
            dma((variables,)),
            pltpu.VMEM((2, SUB, LANES), f32),
            pltpu.VMEM((n_rad, SUB, LANES), f32),
            pltpu.VMEM((n_ax, SUB, LANES), f32),
            dma((2, half, 4)), dma((2, half, 4)),
            dma((n_rad,)), dma((n_rad,)), dma((n_ax,)), dma((n_ax,)),
        ],
        compiler_params=pltpu.CompilerParams(
            collective_id=0, has_side_effects=True, vmem_limit_bytes=64 * 2**20
        ),
    )(forcing.reshape(vectors * cells, LANES), vel_axial, vel_radial, coupling, viscosity)
    return pl.pallas_call(
        functools.partial(finish, sizes),
        out_shape=(
            jax.ShapeDtypeStruct(forcing.shape, f32),
            jax.ShapeDtypeStruct((vectors, vectors), f32),
        ),
        in_specs=[vmem, hbm],
        out_specs=(hbm, vmem),
        scratch_shapes=[
            pltpu.VMEM(split.shape, split.dtype),
            pltpu.VMEM(forcing.shape, f32),
            dma((variables,)), dma((variables,)),
        ],
        compiler_params=pltpu.CompilerParams(vmem_limit_bytes=64 * 2**20),
    )(folded, split)


def solution(mesh):
    return jax.shard_map(
        per_device,
        mesh=mesh,
        in_specs=(
            P(None, None, "ax", "rad"),
            P("ax", "rad"),
            P("ax", "rad"),
            P(None, None, "ax", "rad"),
            P(),
        ),
        out_specs=(P(None, None, "ax", "rad"), P()),
        check_vma=False,
    )
```

```python
import functools

import jax
import jax.numpy as jnp
from jax import lax
from jax.experimental import pallas as pl
from jax.experimental.pallas import tpu as pltpu
from jax.sharding import PartitionSpec as P

STEPS = 3
time_step = 0.8

LANES = 128
SUB = 8
MESH = pl.DeviceIdType.MESH


def kernel(
    sizes, f_ref, va_ref, vr_ref, cp_ref, nu_ref, split_out, folded_ref,
    forcing_in, va_in, vr_in, cp_in, nu_in, in_sem,
    field_0, field_1, coef, packed, from_left, from_right, split, split_sem, mine, rad_slots, ax_slots,
    send_sem, recv_sem, rad_send, rad_recv, ax_send, ax_recv,
):
    vectors, variables, rows, n_ax, n_rad = sizes
    groups = vectors // SUB
    cells = variables * rows
    fields = (field_0, field_1)
    ax = lax.axis_index("ax")
    rad = lax.axis_index("rad")
    ax_before = lax.rem(ax + n_ax - 1, n_ax)
    ax_after = lax.rem(ax + 1, n_ax)
    rad_before = lax.rem(rad + n_rad - 1, n_rad)
    rad_after = lax.rem(rad + 1, n_rad)
    sends = (ax > 0, ax < n_ax - 1, rad > 0, rad < n_rad - 1)
    takes = (ax < n_ax - 1, ax > 0, rad < n_rad - 1, rad > 0)
    lane = lax.broadcasted_iota(jnp.int32, (SUB, LANES), 1)
    sub = lax.broadcasted_iota(jnp.int32, (SUB, LANES), 0)
    slot = lane // 8
    tile = (SUB, LANES)

    def link(buf, g, d):
        if d == 0:
            src, dst = fields[buf].at[g, :, 2:4], fields[buf].at[g, :, rows + 2 : rows + 4]
            device = (ax_before, rad)
        elif d == 1:
            src, dst = fields[buf].at[g, :, rows : rows + 2], fields[buf].at[g, :, 0:2]
            device = (ax_after, rad)
        elif d == 2:
            src, dst = packed.at[buf, g], from_right.at[buf, g]
            device = (ax, rad_before)
        else:
            src, dst = packed.at[buf, g], from_left.at[buf, g]
            device = (ax, rad_after)
        return pltpu.make_async_remote_copy(
            src_ref=src, dst_ref=dst,
            send_sem=send_sem.at[buf, g, d], recv_sem=recv_sem.at[buf, g, d],
            device_id=device, device_id_type=MESH,
        )

    def start(buf, g, d):
        @pl.when(sends[d])
        def _():
            link(buf, g, d).start()

    def wait_send(buf, g, d):
        @pl.when(sends[d])
        def _():
            link(buf, g, d).wait_send()

    def wait_recv(buf, g, d):
        @pl.when(takes[d])
        def _():
            link(buf, g, d).wait_recv()

    part = SUB * cells
    pieces = [
        pltpu.make_async_copy(
            f_ref.at[pl.ds(g * part, part)], forcing_in.at[pl.ds(g * part, part)], in_sem.at[g]
        )
        for g in range(groups)
    ]
    others = [
        pltpu.make_async_copy(source, target, in_sem.at[groups + i])
        for i, (source, target) in enumerate(
            ((va_ref, va_in), (vr_ref, vr_in), (cp_ref, cp_in), (nu_ref, nu_in))
        )
    ]
    for copy in pieces + others:
        copy.start()

    zero_rows = jnp.zeros((variables, 2, SUB, LANES), jnp.float32)
    zero_side = jnp.zeros((variables, SUB, LANES), jnp.float32)
    def clear(g, carry):
        for buf in range(2):
            fields[buf][g, :, 0:2] = zero_rows
            fields[buf][g, :, rows + 2 : rows + 4] = zero_rows
            from_left[buf, g] = zero_side
            from_right[buf, g] = zero_side
        return carry

    lax.fori_loop(0, groups, clear, 0)

    barrier = pltpu.get_barrier_semaphore()
    for step in range(1, n_ax):
        pl.semaphore_signal(
            barrier, inc=1, device_id=(lax.rem(ax + step, n_ax), rad), device_id_type=MESH
        )
    for step in range(1, n_rad):
        pl.semaphore_signal(
            barrier, inc=1, device_id=(ax, lax.rem(rad + step, n_rad)), device_id_type=MESH
        )

    for g in range(groups):
        pieces[g].wait()
        def bring(v, carry):
            pack = jnp.zeros(tile, jnp.float32)
            for a in range(rows):
                value = forcing_in[pl.ds(g * part + v * rows + a, SUB, stride=cells), :]
                field_0[g, v, a + 2] = value
                pack = jnp.where(slot == a, pltpu.roll(value, 2 + 8 * a, 1), pack)
            packed[0, g, v] = pack
            return carry

        lax.fori_loop(0, variables, bring, 0)
        if g == 0:
            pl.semaphore_wait(barrier, n_ax + n_rad - 2)
        for d in range(4):
            start(0, g, d)
    for copy in others:
        copy.wait()

    def prepare(a, carry):
        vel_a = jnp.broadcast_to(va_in[pl.ds(a, 1), :], tile) * (time_step / 12.0)
        vel_r = jnp.broadcast_to(vr_in[pl.ds(a, 1), :], tile) * (time_step / 12.0)
        for v in range(variables):
            nu = jnp.full(tile, nu_in[v], jnp.float32) * (time_step / 12.0)
            terms = []
            for vel in (vel_a, vel_r):
                terms += [16.0 * nu - 8.0 * vel, 16.0 * nu + 8.0 * vel, vel - nu, -vel - nu]
            for w in range(variables):
                term = time_step * jnp.broadcast_to(cp_in[v, w, pl.ds(a, 1), :], tile)
                if w == v:
                    term = term + (1.0 - 60.0 * nu)
                terms.append(term)
            for t, term in enumerate(terms):
                coef[v, a, t] = term
        return carry

    lax.fori_loop(0, rows, prepare, 0)

    block = 4

    def advance(src, g):
        dst = 1 - src
        now, later = fields[src], fields[dst]

        def turn(i, carry):
            sides, packs = carry
            base = block * i
            packs = [pltpu.roll(pack, LANES - 8 * block, 1) for pack in packs]
            done = []
            for k in range(block):
                a = base + k
                at = rows - block + k
                centre = [now[g, v, a + 2] for v in range(variables)]
                for v in range(variables):
                    x = centre[v]
                    side = pltpu.roll(sides[v], LANES - 2 - 8 * k, 1)
                    near = [
                        now[g, v, a + 3],
                        now[g, v, a + 1],
                        now[g, v, a + 4],
                        now[g, v, a],
                        pltpu.roll(jnp.where(lane == 0, side, x), LANES - 1, 1),
                        pltpu.roll(jnp.where(lane == LANES - 1, side, x), 1, 1),
                        pltpu.roll(jnp.where(lane < 2, side, x), LANES - 2, 1),
                        pltpu.roll(jnp.where(lane >= LANES - 2, side, x), 2, 1),
                    ]
                    parts = [coef[v, a, t] * q for t, q in enumerate(near + centre)]
                    while len(parts) > 1:
                        parts = [
                            parts[j] + parts[j + 1] if j + 1 < len(parts) else parts[j]
                            for j in range(0, len(parts), 2)
                        ]
                    new = parts[0]
                    if src == 1:
                        new = 0.5 * (later[g, v, a + 2] + new)
                    done.append((v, a, new))
                    packs[v] = jnp.where(
                        slot == at, pltpu.roll(new, (2 + 8 * at) % LANES, 1), packs[v]
                    )
            for v, a, new in done:
                later[g, v, a + 2] = new
            return [pltpu.roll(side, LANES - 8 * block, 1) for side in sides], packs

        sides = [
            jnp.where(lane % 8 < 2, from_left[src, g, v], from_right[src, g, v])
            for v in range(variables)
        ]
        packs = [jnp.zeros(tile, jnp.float32) for _ in range(variables)]
        _, packs = lax.fori_loop(0, rows // block, turn, (sides, packs))
        for v in range(variables):
            packed[dst, g, v] = packs[v]

    def both_halves(step, carry):
        def half(src):
            more = jnp.logical_or(step < STEPS - 1, src == 0)

            def one_group(g, inner):
                for d in range(4):
                    wait_recv(src, g, d)
                if src == 1:
                    for d in range(4):
                        wait_send(0, g, d)
                else:
                    @pl.when(step > 0)
                    def _():
                        for d in range(4):
                            wait_send(1, g, d)


                def send(directions):
                    @pl.when(more)
                    def _():
                        for d in directions:
                            start(1 - src, g, d)

                advance(src, g)
                send((2, 3, 0, 1))
                return inner

            lax.fori_loop(0, groups, one_group, 0)

        half(0)
        half(1)
        return carry

    lax.fori_loop(0, STEPS, both_halves, 0)

    def drain(g, carry):
        for d in range(4):
            wait_send(1, g, d)
        return carry

    lax.fori_loop(0, groups, drain, 0)

    def leave(v):
        return pltpu.make_async_copy(split.at[v], split_out.at[v], split_sem.at[v])

    def products(v, total):
        for p in range(rows // 2):
            for e in range(2):
                x = jnp.concatenate(
                    [field_0[g, v, 2 * p + e + 2] for g in range(groups)], axis=0
                )
                high = x.astype(jnp.bfloat16)
                low = (x - high.astype(jnp.float32)).astype(jnp.bfloat16)
                split[v, p, :, e * LANES : (e + 1) * LANES] = jnp.concatenate(
                    [high, low, high, low], axis=0
                )
            both = split[v, p]
            total = total + lax.dot_general(
                both[: 2 * vectors], both, (((1,), (1,)), ((), ())),
                preferred_element_type=jnp.float32,
            )
        leave(v).start()
        return total

    total = lax.fori_loop(
        0, variables, products, jnp.zeros((2 * vectors, LANES), jnp.float32)
    )
    half_sum = total[:vectors] + total[vectors:]
    gram = half_sum + pltpu.roll(half_sum, vectors, 1)
    gram = gram * (1.0 / (cells * LANES * n_ax * n_rad))
    quarter = lane // vectors
    folded = gram[:SUB]
    for i in range(1, vectors // SUB):
        folded = jnp.where(quarter == i, gram[SUB * i : SUB * (i + 1)], folded)

    def sum_over(value, n, me, place, slots, sends_on, takes_on, held):
        held[...] = value
        copies = []
        for step in range(1, n):
            copy = pltpu.make_async_remote_copy(
                src_ref=held, dst_ref=slots.at[me],
                send_sem=sends_on.at[step], recv_sem=takes_on.at[step],
                device_id=place(lax.rem(me + step, n)), device_id_type=MESH,
            )
            copy.start()
            copies.append(copy)
        slots[me] = value
        for copy in copies:
            copy.wait_send()
            copy.wait_recv()
        result = slots[0]
        for i in range(1, n):
            result = result + slots[i]
        return result

    folded = sum_over(
        folded, n_rad, rad, lambda i: (ax, i), rad_slots, rad_send, rad_recv, mine.at[0]
    )
    folded = sum_over(
        folded, n_ax, ax, lambda i: (i, rad), ax_slots, ax_send, ax_recv, mine.at[1]
    )

    folded_ref[...] = folded
    for v in range(variables):
        leave(v).wait()


def finish(sizes, folded_ref, split_in, out_ref, r_ref, split, basis, in_sem, out_sem):
    vectors, variables, rows, n_ax, n_rad = sizes
    lane = lax.broadcasted_iota(jnp.int32, (SUB, LANES), 1)
    sub = lax.broadcasted_iota(jnp.int32, (SUB, LANES), 0)
    quarter = lane // vectors
    tile = (SUB, LANES)
    folded = folded_ref[...]

    def enter(v):
        return pltpu.make_async_copy(split_in.at[v], split.at[v], in_sem.at[v])

    for v in range(variables):
        enter(v).start()

    blocks = []
    for b in range(vectors // SUB):
        part = folded if b == 0 else pltpu.roll(folded, LANES - vectors * b, 1)
        unit = jnp.where(lane - vectors == sub + SUB * b, 1.0, 0.0)
        blocks.append(jnp.where(lane < vectors, part, unit))
    for j in range(0, vectors, 2):
        jb, js = j // SUB, j % SUB
        below = range(jb, len(blocks))
        first = jnp.broadcast_to(blocks[jb][js : js + 1, :], tile)
        second = jnp.broadcast_to(blocks[jb][js + 1 : js + 2, :], tile)
        column = {b: jnp.broadcast_to(blocks[b][:, j : j + 1], tile) for b in below}
        other = {b: jnp.broadcast_to(blocks[b][:, j + 1 : j + 2], tile) for b in below}

        def entry(columns, i):
            return jnp.broadcast_to(columns[jb][i : i + 1, :], tile)

        over = 1.0 / entry(column, js)
        ratio = entry(column, js + 1) * over
        across = entry(other, js) * over
        last = 1.0 / (entry(other, js + 1) - ratio * entry(other, js))
        first_scaled = first * over
        second_scaled = (second - ratio * first) * last
        for b in below:
            change = column[b] * first_scaled
            more = (other[b] - column[b] * across) * second_scaled
            if b == jb:
                change = jnp.where(sub > js, change, 0.0)
                more = jnp.where(sub > js + 1, more, 0.0)
            blocks[b] = blocks[b] - change - more
    lefts, rights = [], []
    for b, block in enumerate(blocks):
        diagonal = jnp.sum(
            jnp.where(lane == sub + SUB * b, block, 0.0), axis=1, keepdims=True
        )
        block = block * (1.0 / jnp.sqrt(jnp.broadcast_to(diagonal, tile)))
        lefts.append(jnp.where(lane >= sub + SUB * b, block, 0.0))
        inverse = jnp.where(quarter == 1, block, 0.0)
        inverse = inverse + pltpu.roll(inverse, vectors, 1)
        inverse = inverse + pltpu.roll(inverse, 2 * vectors, 1)
        rights.append(inverse)
    r_ref[...] = jnp.concatenate(lefts, axis=0)[:, :vectors]
    inverse = jnp.concatenate(rights, axis=0)
    high = inverse.astype(jnp.bfloat16).astype(jnp.float32)
    wide = lax.broadcasted_iota(jnp.int32, (vectors, LANES), 1)
    factors = jnp.where(wide < 2 * vectors, high, inverse - high).astype(jnp.bfloat16)

    def leave(v):
        return pltpu.make_async_copy(
            basis.at[:, v], out_ref.at[:, v], out_sem.at[v]
        )

    def outputs(v, carry):
        enter(v).wait()
        for p in range(rows // 2):
            found = jnp.dot(factors, split[v, p], preferred_element_type=jnp.float32)
            for e in range(2):
                basis[:, v, 2 * p + e, :] = found[:, e * LANES : (e + 1) * LANES]
        leave(v).start()
        return carry

    lax.fori_loop(0, variables, outputs, 0)
    for v in range(variables):
        leave(v).wait()


def per_device(forcing, vel_axial, vel_radial, coupling, viscosity):
    vectors, variables, rows, columns = forcing.shape
    n_ax, n_rad = lax.axis_size("ax"), lax.axis_size("rad")
    groups = vectors // SUB
    cells = variables * rows
    assert columns == LANES and rows * 8 == LANES and vectors * 4 == LANES
    f32 = jnp.float32
    vmem = pl.BlockSpec(memory_space=pltpu.VMEM)
    side = pltpu.VMEM((2, groups, variables, SUB, LANES), f32)
    field = pltpu.VMEM((groups, variables, rows + 4, SUB, LANES), f32)
    dma = pltpu.SemaphoreType.DMA
    sizes = (vectors, variables, rows, n_ax, n_rad)
    hbm = pl.BlockSpec(memory_space=pltpu.HBM)
    split, folded = pl.pallas_call(
        functools.partial(kernel, sizes),
        out_shape=(
            jax.ShapeDtypeStruct((variables, rows // 2, LANES, 2 * LANES), jnp.bfloat16),
            jax.ShapeDtypeStruct((SUB, LANES), f32),
        ),
        in_specs=[hbm] * 5,
        out_specs=(hbm, vmem),
        scratch_shapes=[
            pltpu.VMEM((vectors * cells, LANES), f32),
            pltpu.VMEM((rows, LANES), f32),
            pltpu.VMEM((rows, LANES), f32),
            pltpu.VMEM((variables, variables, rows, LANES), f32),
            pltpu.SMEM((variables,), f32),
            dma((groups + 4,)),
            field, field,
            pltpu.VMEM((variables, rows, 8 + variables, SUB, LANES), f32),
            side, side, side,
            pltpu.VMEM((variables, rows // 2, LANES, 2 * LANES), jnp.bfloat16),
            dma((variables,)),
            pltpu.VMEM((2, SUB, LANES), f32),
            pltpu.VMEM((n_rad, SUB, LANES), f32),
            pltpu.VMEM((n_ax, SUB, LANES), f32),
            dma((2, groups, 4)), dma((2, groups, 4)),
            dma((n_rad,)), dma((n_rad,)), dma((n_ax,)), dma((n_ax,)),
        ],
        compiler_params=pltpu.CompilerParams(
            collective_id=0, has_side_effects=True, vmem_limit_bytes=64 * 2**20
        ),
    )(forcing.reshape(vectors * cells, LANES), vel_axial, vel_radial, coupling, viscosity)
    return pl.pallas_call(
        functools.partial(finish, sizes),
        out_shape=(
            jax.ShapeDtypeStruct(forcing.shape, f32),
            jax.ShapeDtypeStruct((vectors, vectors), f32),
        ),
        in_specs=[vmem, hbm],
        out_specs=(hbm, vmem),
        scratch_shapes=[
            pltpu.VMEM(split.shape, split.dtype),
            pltpu.VMEM(forcing.shape, f32),
            dma((variables,)), dma((variables,)),
        ],
        compiler_params=pltpu.CompilerParams(vmem_limit_bytes=64 * 2**20),
    )(folded, split)


def solution(mesh):
    return jax.shard_map(
        per_device,
        mesh=mesh,
        in_specs=(
            P(None, None, "ax", "rad"),
            P("ax", "rad"),
            P("ax", "rad"),
            P(None, None, "ax", "rad"),
            P(),
        ),
        out_specs=(P(None, None, "ax", "rad"), P()),
        check_vma=False,
    )
```

```python
import functools

import jax
import jax.numpy as jnp
from jax import lax
from jax.experimental import pallas as pl
from jax.experimental.pallas import tpu as pltpu
from jax.sharding import PartitionSpec as P

STEPS = 3
time_step = 0.8

LANES = 128
SUB = 8
MESH = pl.DeviceIdType.MESH


def kernel(
    sizes, f_ref, va_ref, vr_ref, cp_ref, nu_ref, split_out, folded_ref,
    forcing_in, va_in, vr_in, cp_in, nu_in, in_sem,
    field_0, field_1, coef, packed, from_left, from_right, split, split_sem, mine, rad_slots, ax_slots,
    send_sem, recv_sem, rad_send, rad_recv, ax_send, ax_recv,
):
    vectors, variables, rows, n_ax, n_rad = sizes
    groups = vectors // SUB
    cells = variables * rows
    fields = (field_0, field_1)
    ax = lax.axis_index("ax")
    rad = lax.axis_index("rad")
    ax_before = lax.rem(ax + n_ax - 1, n_ax)
    ax_after = lax.rem(ax + 1, n_ax)
    rad_before = lax.rem(rad + n_rad - 1, n_rad)
    rad_after = lax.rem(rad + 1, n_rad)
    sends = (ax > 0, ax < n_ax - 1, rad > 0, rad < n_rad - 1)
    takes = (ax < n_ax - 1, ax > 0, rad < n_rad - 1, rad > 0)
    lane = lax.broadcasted_iota(jnp.int32, (SUB, LANES), 1)
    sub = lax.broadcasted_iota(jnp.int32, (SUB, LANES), 0)
    slot = lane // 8
    tile = (SUB, LANES)

    def link(buf, g, d):
        if d == 0:
            src, dst = fields[buf].at[g, :, 2:4], fields[buf].at[g, :, rows + 2 : rows + 4]
            device = (ax_before, rad)
        elif d == 1:
            src, dst = fields[buf].at[g, :, rows : rows + 2], fields[buf].at[g, :, 0:2]
            device = (ax_after, rad)
        elif d == 2:
            src, dst = packed.at[buf, g], from_right.at[buf, g]
            device = (ax, rad_before)
        else:
            src, dst = packed.at[buf, g], from_left.at[buf, g]
            device = (ax, rad_after)
        return pltpu.make_async_remote_copy(
            src_ref=src, dst_ref=dst,
            send_sem=send_sem.at[buf, g, d], recv_sem=recv_sem.at[buf, g, d],
            device_id=device, device_id_type=MESH,
        )

    def start(buf, g, d):
        @pl.when(sends[d])
        def _():
            link(buf, g, d).start()

    def wait_send(buf, g, d):
        @pl.when(sends[d])
        def _():
            link(buf, g, d).wait_send()

    def wait_recv(buf, g, d):
        @pl.when(takes[d])
        def _():
            link(buf, g, d).wait_recv()

    part = SUB * cells
    pieces = [
        pltpu.make_async_copy(
            f_ref.at[pl.ds(g * part, part)], forcing_in.at[pl.ds(g * part, part)], in_sem.at[g]
        )
        for g in range(groups)
    ]
    others = [
        pltpu.make_async_copy(source, target, in_sem.at[groups + i])
        for i, (source, target) in enumerate(
            ((va_ref, va_in), (vr_ref, vr_in), (cp_ref, cp_in), (nu_ref, nu_in))
        )
    ]
    for copy in pieces + others:
        copy.start()

    zero_rows = jnp.zeros((variables, 2, SUB, LANES), jnp.float32)
    zero_side = jnp.zeros((variables, SUB, LANES), jnp.float32)
    def clear(g, carry):
        for buf in range(2):
            fields[buf][g, :, 0:2] = zero_rows
            fields[buf][g, :, rows + 2 : rows + 4] = zero_rows
            from_left[buf, g] = zero_side
            from_right[buf, g] = zero_side
        return carry

    lax.fori_loop(0, groups, clear, 0)

    barrier = pltpu.get_barrier_semaphore()
    for step in range(1, n_ax):
        pl.semaphore_signal(
            barrier, inc=1, device_id=(lax.rem(ax + step, n_ax), rad), device_id_type=MESH
        )
    for step in range(1, n_rad):
        pl.semaphore_signal(
            barrier, inc=1, device_id=(ax, lax.rem(rad + step, n_rad)), device_id_type=MESH
        )

    for g in range(groups):
        pieces[g].wait()
        def bring(v, carry):
            pack = jnp.zeros(tile, jnp.float32)
            for a in range(rows):
                value = forcing_in[pl.ds(g * part + v * rows + a, SUB, stride=cells), :]
                field_0[g, v, a + 2] = value
                pack = jnp.where(slot == a, pltpu.roll(value, 2 + 8 * a, 1), pack)
            packed[0, g, v] = pack
            return carry

        lax.fori_loop(0, variables, bring, 0)
        if g == 0:
            pl.semaphore_wait(barrier, n_ax + n_rad - 2)
        for d in range(4):
            start(0, g, d)
    for copy in others:
        copy.wait()

    def prepare(a, carry):
        vel_a = jnp.broadcast_to(va_in[pl.ds(a, 1), :], tile) * (time_step / 12.0)
        vel_r = jnp.broadcast_to(vr_in[pl.ds(a, 1), :], tile) * (time_step / 12.0)
        for v in range(variables):
            nu = jnp.full(tile, nu_in[v], jnp.float32) * (time_step / 12.0)
            terms = []
            for vel in (vel_a, vel_r):
                terms += [16.0 * nu - 8.0 * vel, 16.0 * nu + 8.0 * vel, vel - nu, -vel - nu]
            for w in range(variables):
                term = time_step * jnp.broadcast_to(cp_in[v, w, pl.ds(a, 1), :], tile)
                if w == v:
                    term = term + (1.0 - 60.0 * nu)
                terms.append(term)
            for t, term in enumerate(terms):
                coef[v, a, t] = term
        return carry

    lax.fori_loop(0, rows, prepare, 0)

    block = 4
    turns = rows // block

    def advance(src, g, start_axial):
        dst = 1 - src
        now, later = fields[src], fields[dst]

        def turn(i, carry):
            sides, packs = carry
            base = block * ((i + turns - 1) % turns)
            packs = [pltpu.roll(pack, LANES - 8 * block, 1) for pack in packs]
            done = []
            for k in range(block):
                a = base + k
                at = rows - block + k
                centre = [now[g, v, a + 2] for v in range(variables)]
                for v in range(variables):
                    x = centre[v]
                    side = pltpu.roll(sides[v], LANES - 2 - 8 * k, 1)
                    near = [
                        now[g, v, a + 3],
                        now[g, v, a + 1],
                        now[g, v, a + 4],
                        now[g, v, a],
                        pltpu.roll(jnp.where(lane == 0, side, x), LANES - 1, 1),
                        pltpu.roll(jnp.where(lane == LANES - 1, side, x), 1, 1),
                        pltpu.roll(jnp.where(lane < 2, side, x), LANES - 2, 1),
                        pltpu.roll(jnp.where(lane >= LANES - 2, side, x), 2, 1),
                    ]
                    parts = [coef[v, a, t] * q for t, q in enumerate(near + centre)]
                    while len(parts) > 1:
                        parts = [
                            parts[j] + parts[j + 1] if j + 1 < len(parts) else parts[j]
                            for j in range(0, len(parts), 2)
                        ]
                    new = parts[0]
                    if src == 1:
                        new = 0.5 * (later[g, v, a + 2] + new)
                    done.append((v, a, new))
                    packs[v] = jnp.where(
                        slot == at, pltpu.roll(new, (2 + 8 * at) % LANES, 1), packs[v]
                    )
            for v, a, new in done:
                later[g, v, a + 2] = new

            @pl.when(i == 1)
            def _():
                start_axial()

            return [pltpu.roll(side, LANES - 8 * block, 1) for side in sides], packs

        sides = [
            pltpu.roll(
                jnp.where(lane % 8 < 2, from_left[src, g, v], from_right[src, g, v]),
                8 * block, 1,
            )
            for v in range(variables)
        ]
        packs = [jnp.zeros(tile, jnp.float32) for _ in range(variables)]
        _, packs = lax.fori_loop(0, turns, turn, (sides, packs))
        for v in range(variables):
            packed[dst, g, v] = pltpu.roll(packs[v], LANES - 8 * block, 1)

    def both_halves(step, carry):
        def half(src):
            more = jnp.logical_or(step < STEPS - 1, src == 0)

            def one_group(g, inner):
                for d in range(4):
                    wait_recv(src, g, d)
                if src == 1:
                    for d in range(4):
                        wait_send(0, g, d)
                else:
                    @pl.when(step > 0)
                    def _():
                        for d in range(4):
                            wait_send(1, g, d)


                def send(directions):
                    @pl.when(more)
                    def _():
                        for d in directions:
                            start(1 - src, g, d)

                advance(src, g, lambda: send((0, 1)))
                send((2, 3))
                return inner

            lax.fori_loop(0, groups, one_group, 0)

        half(0)
        half(1)
        return carry

    lax.fori_loop(0, STEPS, both_halves, 0)

    def drain(g, carry):
        for d in range(4):
            wait_send(1, g, d)
        return carry

    lax.fori_loop(0, groups, drain, 0)

    def leave(v):
        return pltpu.make_async_copy(split.at[v], split_out.at[v], split_sem.at[v])

    def products(v, total):
        for p in range(rows // 2):
            for e in range(2):
                x = jnp.concatenate(
                    [field_0[g, v, 2 * p + e + 2] for g in range(groups)], axis=0
                )
                high = x.astype(jnp.bfloat16)
                low = (x - high.astype(jnp.float32)).astype(jnp.bfloat16)
                split[v, p, :, e * LANES : (e + 1) * LANES] = jnp.concatenate(
                    [high, low, high, low], axis=0
                )
            both = split[v, p]
            total = total + lax.dot_general(
                both[: 2 * vectors], both, (((1,), (1,)), ((), ())),
                preferred_element_type=jnp.float32,
            )
        leave(v).start()
        return total

    total = lax.fori_loop(
        0, variables, products, jnp.zeros((2 * vectors, LANES), jnp.float32)
    )
    half_sum = total[:vectors] + total[vectors:]
    gram = half_sum + pltpu.roll(half_sum, vectors, 1)
    gram = gram * (1.0 / (cells * LANES * n_ax * n_rad))
    quarter = lane // vectors
    folded = gram[:SUB]
    for i in range(1, vectors // SUB):
        folded = jnp.where(quarter == i, gram[SUB * i : SUB * (i + 1)], folded)

    def sum_over(value, n, me, place, slots, sends_on, takes_on, held):
        held[...] = value
        copies = []
        for step in range(1, n):
            copy = pltpu.make_async_remote_copy(
                src_ref=held, dst_ref=slots.at[me],
                send_sem=sends_on.at[step], recv_sem=takes_on.at[step],
                device_id=place(lax.rem(me + step, n)), device_id_type=MESH,
            )
            copy.start()
            copies.append(copy)
        slots[me] = value
        for copy in copies:
            copy.wait_send()
            copy.wait_recv()
        result = slots[0]
        for i in range(1, n):
            result = result + slots[i]
        return result

    folded = sum_over(
        folded, n_rad, rad, lambda i: (ax, i), rad_slots, rad_send, rad_recv, mine.at[0]
    )
    folded = sum_over(
        folded, n_ax, ax, lambda i: (i, rad), ax_slots, ax_send, ax_recv, mine.at[1]
    )

    folded_ref[...] = folded
    for v in range(variables):
        leave(v).wait()


def finish(sizes, folded_ref, split_in, out_ref, r_ref, split, basis, in_sem, out_sem):
    vectors, variables, rows, n_ax, n_rad = sizes
    lane = lax.broadcasted_iota(jnp.int32, (SUB, LANES), 1)
    sub = lax.broadcasted_iota(jnp.int32, (SUB, LANES), 0)
    quarter = lane // vectors
    tile = (SUB, LANES)
    folded = folded_ref[...]

    def enter(v):
        return pltpu.make_async_copy(split_in.at[v], split.at[v], in_sem.at[v])

    for v in range(variables):
        enter(v).start()

    blocks = []
    for b in range(vectors // SUB):
        part = folded if b == 0 else pltpu.roll(folded, LANES - vectors * b, 1)
        unit = jnp.where(lane - vectors == sub + SUB * b, 1.0, 0.0)
        blocks.append(jnp.where(lane < vectors, part, unit))
    count = len(blocks)

    def eight_rows(i, blocks):
        blocks = list(blocks)
        for js in range(0, SUB, 2):
            jb, j = 0, js
            below = range(len(blocks))
            first = jnp.broadcast_to(blocks[jb][js : js + 1, :], tile)
            second = jnp.broadcast_to(blocks[jb][js + 1 : js + 2, :], tile)
            column = {b: jnp.broadcast_to(blocks[b][:, j : j + 1], tile) for b in below}
            other = {b: jnp.broadcast_to(blocks[b][:, j + 1 : j + 2], tile) for b in below}

            def entry(columns, i):
                return jnp.broadcast_to(columns[jb][i : i + 1, :], tile)

            over = 1.0 / entry(column, js)
            ratio = entry(column, js + 1) * over
            across = entry(other, js) * over
            last = 1.0 / (entry(other, js + 1) - ratio * entry(other, js))
            first_scaled = first * over
            second_scaled = (second - ratio * first) * last
            for b in below:
                change = column[b] * first_scaled
                more = (other[b] - column[b] * across) * second_scaled
                if b == jb:
                    change = jnp.where(sub > js, change, 0.0)
                    more = jnp.where(sub > js + 1, more, 0.0)
                else:
                    change = jnp.where(b < count - i, change + more, 0.0)
                    more = 0.0
                blocks[b] = blocks[b] - change - more
        blocks = [pltpu.roll(block, LANES - SUB, 1) for block in blocks]
        return blocks[1:] + blocks[:1]

    blocks = lax.fori_loop(0, count, eight_rows, blocks)
    blocks = [pltpu.roll(block, vectors, 1) for block in blocks]
    lefts, rights = [], []
    for b, block in enumerate(blocks):
        diagonal = jnp.sum(
            jnp.where(lane == sub + SUB * b, block, 0.0), axis=1, keepdims=True
        )
        block = block * (1.0 / jnp.sqrt(jnp.broadcast_to(diagonal, tile)))
        lefts.append(jnp.where(lane >= sub + SUB * b, block, 0.0))
        inverse = jnp.where(quarter == 1, block, 0.0)
        inverse = inverse + pltpu.roll(inverse, vectors, 1)
        inverse = inverse + pltpu.roll(inverse, 2 * vectors, 1)
        rights.append(inverse)
    r_ref[...] = jnp.concatenate(lefts, axis=0)[:, :vectors]
    inverse = jnp.concatenate(rights, axis=0)
    high = inverse.astype(jnp.bfloat16).astype(jnp.float32)
    wide = lax.broadcasted_iota(jnp.int32, (vectors, LANES), 1)
    factors = jnp.where(wide < 2 * vectors, high, inverse - high).astype(jnp.bfloat16)

    def leave(v):
        return pltpu.make_async_copy(
            basis.at[:, v], out_ref.at[:, v], out_sem.at[v]
        )

    def outputs(v, carry):
        enter(v).wait()
        for p in range(rows // 2):
            found = jnp.dot(factors, split[v, p], preferred_element_type=jnp.float32)
            for e in range(2):
                basis[:, v, 2 * p + e, :] = found[:, e * LANES : (e + 1) * LANES]
        leave(v).start()
        return carry

    lax.fori_loop(0, variables, outputs, 0)
    for v in range(variables):
        leave(v).wait()


def per_device(forcing, vel_axial, vel_radial, coupling, viscosity):
    vectors, variables, rows, columns = forcing.shape
    n_ax, n_rad = lax.axis_size("ax"), lax.axis_size("rad")
    groups = vectors // SUB
    cells = variables * rows
    assert columns == LANES and rows * 8 == LANES and vectors * 4 == LANES
    f32 = jnp.float32
    vmem = pl.BlockSpec(memory_space=pltpu.VMEM)
    side = pltpu.VMEM((2, groups, variables, SUB, LANES), f32)
    field = pltpu.VMEM((groups, variables, rows + 4, SUB, LANES), f32)
    dma = pltpu.SemaphoreType.DMA
    sizes = (vectors, variables, rows, n_ax, n_rad)
    hbm = pl.BlockSpec(memory_space=pltpu.HBM)
    split, folded = pl.pallas_call(
        functools.partial(kernel, sizes),
        out_shape=(
            jax.ShapeDtypeStruct((variables, rows // 2, LANES, 2 * LANES), jnp.bfloat16),
            jax.ShapeDtypeStruct((SUB, LANES), f32),
        ),
        in_specs=[hbm] * 5,
        out_specs=(hbm, vmem),
        scratch_shapes=[
            pltpu.VMEM((vectors * cells, LANES), f32),
            pltpu.VMEM((rows, LANES), f32),
            pltpu.VMEM((rows, LANES), f32),
            pltpu.VMEM((variables, variables, rows, LANES), f32),
            pltpu.SMEM((variables,), f32),
            dma((groups + 4,)),
            field, field,
            pltpu.VMEM((variables, rows, 8 + variables, SUB, LANES), f32),
            side, side, side,
            pltpu.VMEM((variables, rows // 2, LANES, 2 * LANES), jnp.bfloat16),
            dma((variables,)),
            pltpu.VMEM((2, SUB, LANES), f32),
            pltpu.VMEM((n_rad, SUB, LANES), f32),
            pltpu.VMEM((n_ax, SUB, LANES), f32),
            dma((2, groups, 4)), dma((2, groups, 4)),
            dma((n_rad,)), dma((n_rad,)), dma((n_ax,)), dma((n_ax,)),
        ],
        compiler_params=pltpu.CompilerParams(
            collective_id=0, has_side_effects=True, vmem_limit_bytes=64 * 2**20
        ),
    )(forcing.reshape(vectors * cells, LANES), vel_axial, vel_radial, coupling, viscosity)
    return pl.pallas_call(
        functools.partial(finish, sizes),
        out_shape=(
            jax.ShapeDtypeStruct(forcing.shape, f32),
            jax.ShapeDtypeStruct((vectors, vectors), f32),
        ),
        in_specs=[vmem, hbm],
        out_specs=(hbm, vmem),
        scratch_shapes=[
            pltpu.VMEM(split.shape, split.dtype),
            pltpu.VMEM(forcing.shape, f32),
            dma((variables,)), dma((variables,)),
        ],
        compiler_params=pltpu.CompilerParams(vmem_limit_bytes=64 * 2**20),
    )(folded, split)


def solution(mesh):
    return jax.shard_map(
        per_device,
        mesh=mesh,
        in_specs=(
            P(None, None, "ax", "rad"),
            P("ax", "rad"),
            P("ax", "rad"),
            P(None, None, "ax", "rad"),
            P(),
        ),
        out_specs=(P(None, None, "ax", "rad"), P()),
        check_vma=False,
    )
```
